32 devices in a mesh: blk: 8 (over y, x, core), dp: 4 (over z).
Axes of the slice: x: 2, y: 2, z: 4, core: 2. Of those that a mesh axis runs over, the one named last changes fastest.
Arguments:
- inputs: bfloat16 [1024, 2560], P('blk'), may hold values from -400 to 400
- gain: float32 [2560], replicated, may hold values from 0.1 to 1.9
- w_gate: bfloat16 [2560, 6912], P('blk', 'dp'), may hold values from -0.125 to 0.125
- w_up: bfloat16 [2560, 6912], P('blk', 'dp'), may hold values from -0.125 to 0.125
- upstream: bfloat16 [1024, 6912], P('blk', 'dp'), may hold values from -6 to 6
Outputs:
- hidden: bfloat16 [1024, 6912], P('blk', 'dp')
- grad_gate: float32 [2560, 6912], P('blk', 'dp')
- grad_up: float32 [2560, 6912], P('blk', 'dp')
- grad_input: bfloat16 [1024, 2560], P('blk', 'dp')
- grad_gain: float32 [2560], P('dp')
The draws below stay inside these ranges and needn't reach their ends.
All inputs are finite; a program needn't handle non-finite values.
Results may differ from the reference program's by a relative error of at most 0.028.
Values may be sent and summed in bfloat16 or wider, within the bound.
A program may use at most 64 MiB of HBM per device.

```python
import math
import jax
import jax.numpy as jnp
from jax import lax

D = 2560
FF_WIN = 6912
TOKENS = 1024
N_DP = 4


def draw_inputs(key, part):
    key = jax.random.fold_in(key, 11)
    base_key, row_key, col_key = jax.random.split(key, 3)
    row_scale = jnp.exp(jax.random.uniform(row_key, (TOKENS, 1), jnp.float32) * math.log(10.0))
    col_scale = jnp.exp(jax.random.uniform(col_key, (1, D), jnp.float32) * math.log(10.0))
    base = jnp.clip(jax.random.normal(base_key, (TOKENS, D), jnp.float32), -3.9, 3.9)
    return (base * row_scale * col_scale).astype(jnp.bfloat16)


def shard_levels(own_key, extent, cuts, low, high):
    level = 1.0
    for position, parts in cuts:
        draws = jax.random.uniform(jax.random.fold_in(jax.random.fold_in(own_key, 6), position), (parts,), jnp.float32, low / len(cuts), high / len(cuts))
        level = level * jnp.repeat(jnp.exp(draws), extent[position] // parts).reshape((-1,) + (1,) * (len(extent) - 1 - position))
    return level


def normal_values(key, extent, width, most, cuts=(), dtype=jnp.bfloat16):
    result = width * jax.random.normal(key, extent, jnp.float32)
    if cuts:
        result = result * shard_levels(key, extent, cuts, -0.22, 0.18)
    return jnp.clip(result, -most, most).astype(dtype)


def setup_inputs(seed: int = 0) -> dict:
    keys = jax.random.split(jax.random.key(seed), 6)
    return {
        "inputs": draw_inputs(jax.random.fold_in(keys[5], 71), 0),
        "gain": jnp.clip(1.0 + 0.18 * jax.random.normal(keys[1], (D,), jnp.float32), 0.1, 1.9),
        "w_gate": normal_values(keys[2], (D, FF_WIN), D ** -0.5, 0.125, ((0, 8), (1, 4))),
        "w_up": normal_values(keys[3], (D, FF_WIN), D ** -0.5, 0.125, ((0, 8), (1, 4))),
        "upstream": normal_values(keys[4], (TOKENS, FF_WIN), 1.0, 6.0, ((0, 8), (1, 4))),
    }


def reference(inputs, gain, w_gate, w_up, upstream):
    wide_input = inputs.astype(jnp.float32)
    root_mean = jnp.sqrt(lax.optimization_barrier(jnp.mean(wide_input * wide_input, axis=1, keepdims=True)) + 1e-05)
    unit_input = wide_input / root_mean
    normed = (unit_input * gain).astype(jnp.bfloat16)
    gate_pre = jnp.dot(normed, w_gate, preferred_element_type=jnp.float32)
    up_pre = jnp.dot(normed, w_up, preferred_element_type=jnp.float32)
    sigmoid_gate = jax.nn.sigmoid(gate_pre)
    activated = gate_pre * sigmoid_gate
    hidden = (activated * up_pre).astype(jnp.bfloat16)
    upstream_wide = upstream.astype(jnp.float32)
    back_up = (upstream_wide * activated).astype(jnp.bfloat16)
    back_gate = (upstream_wide * up_pre * sigmoid_gate * (1.0 + gate_pre * (1.0 - sigmoid_gate))).astype(jnp.bfloat16)
    grad_gate = jnp.dot(normed.T, back_gate, preferred_element_type=jnp.float32)
    grad_up = jnp.dot(normed.T, back_up, preferred_element_type=jnp.float32)
    group_cols = w_gate.shape[1] // N_DP
    back_normed = jnp.zeros((inputs.shape[0], inputs.shape[1]), jnp.float32)
    for group in range(N_DP):
        lower = group * group_cols
        upper = lower + group_cols
        group_part = jnp.dot(back_gate[:, lower:upper], w_gate[:, lower:upper].T, preferred_element_type=jnp.float32) + jnp.dot(back_up[:, lower:upper], w_up[:, lower:upper].T, preferred_element_type=jnp.float32)
        rounded = lax.optimization_barrier(group_part.astype(jnp.bfloat16))
        back_normed = back_normed + rounded.astype(jnp.float32)
    token_dots = lax.optimization_barrier(jnp.sum(back_normed * gain * unit_input, axis=1, keepdims=True))
    grad_input = ((back_normed * gain - unit_input * token_dots / inputs.shape[1]) / root_mean).astype(jnp.bfloat16)
    grad_gain = lax.optimization_barrier(jnp.sum(back_normed * unit_input, axis=0))
    return (hidden, grad_gate, grad_up, grad_input, grad_gain)
```

```python
import jax
import jax.numpy as jnp
from jax import lax
from jax.sharding import PartitionSpec as P


def per_device(inputs, gain, w_gate, w_up, upstream):
    wide_input = inputs.astype(jnp.float32)
    root_mean = jnp.sqrt(jnp.mean(wide_input * wide_input, axis=1, keepdims=True) + 1e-05)
    unit_input = wide_input / root_mean
    normed = (unit_input * gain).astype(jnp.bfloat16)
    columns = lax.all_to_all(normed, "blk", split_axis=1, concat_axis=0, tiled=True)
    gate_part = jnp.dot(columns, w_gate, preferred_element_type=jnp.float32).astype(jnp.bfloat16)
    up_part = jnp.dot(columns, w_up, preferred_element_type=jnp.float32).astype(jnp.bfloat16)
    gate_pre = lax.psum_scatter(gate_part, "blk", scatter_dimension=0, tiled=True).astype(jnp.float32)
    up_pre = lax.psum_scatter(up_part, "blk", scatter_dimension=0, tiled=True).astype(jnp.float32)
    sigmoid_gate = jax.nn.sigmoid(gate_pre)
    activated = gate_pre * sigmoid_gate
    hidden = (activated * up_pre).astype(jnp.bfloat16)
    upstream_wide = upstream.astype(jnp.float32)
    back_up = (upstream_wide * activated).astype(jnp.bfloat16)
    back_gate = (
        upstream_wide * up_pre * sigmoid_gate * (1.0 + gate_pre * (1.0 - sigmoid_gate))
    ).astype(jnp.bfloat16)
    all_up = lax.all_gather(back_up, "blk", axis=0, tiled=True)
    all_gate = lax.all_gather(back_gate, "blk", axis=0, tiled=True)
    over_tokens = (((0,), (0,)), ((), ()))
    over_hidden = (((1,), (1,)), ((), ()))
    grad_up = lax.dot_general(columns, all_up, over_tokens, preferred_element_type=jnp.float32)
    grad_gate = lax.dot_general(columns, all_gate, over_tokens, preferred_element_type=jnp.float32)
    part = lax.dot_general(
        all_gate, w_gate, over_hidden, preferred_element_type=jnp.float32
    ) + lax.dot_general(all_up, w_up, over_hidden, preferred_element_type=jnp.float32)
    part = lax.all_to_all(
        part.astype(jnp.bfloat16), "blk", split_axis=0, concat_axis=1, tiled=True
    )
    feature_count = inputs.shape[1] // lax.axis_size("dp")
    feature_start = lax.axis_index("dp") * feature_count
    gain_slice = lax.dynamic_slice_in_dim(gain, feature_start, feature_count, 0)
    unit_slice = lax.dynamic_slice_in_dim(unit_input, feature_start, feature_count, 1)
    own_sums = lax.psum_scatter(part, "dp", scatter_dimension=1, tiled=True).astype(jnp.float32)
    token_totals = lax.psum(jnp.sum(own_sums * gain_slice * unit_slice, axis=1), "dp")
    token_means = token_totals[:, None] / inputs.shape[1]
    grad_input = ((own_sums * gain_slice - unit_slice * token_means) / root_mean).astype(
        jnp.bfloat16
    )
    grad_gain = lax.psum(jnp.sum(own_sums * unit_slice, axis=0), "blk")
    return (hidden, grad_gate, grad_up, grad_input, grad_gain)


def solution(mesh):
    return jax.shard_map(
        per_device,
        mesh=mesh,
        in_specs=(P("blk", None), P(), P("blk", "dp"), P("blk", "dp"), P("blk", "dp")),
        out_specs=(P("blk", "dp"), P("blk", "dp"), P("blk", "dp"), P("blk", "dp"), P("dp")),
        check_vma=False,
    )
```

```python
import functools

import jax
import jax.numpy as jnp
from jax import lax
from jax.experimental import pallas as pl
from jax.experimental.pallas import tpu as pltpu
from jax.sharding import PartitionSpec as P

MESH = pl.DeviceIdType.MESH
ROWS = 16
TILE = 256
DIAG, ACROSS_X, ACROSS_Y, OWN = 6, 2, 4, 0
DIRECTION = (ACROSS_X, ACROSS_Y)


def plane_kernel(
    dp, x_ref, gain_ref, wg_ref, wu_ref, up_ref,
    hid_ref, gg_ref, gu_ref, gi_ref, ggain_ref,
    nb, un, rm, xs, xt, pb, rc, sbuf, rbuf, full, ps, pr, zr, dots, dotr, gsum, gsend,
    x_s, x_r, c_s, c_r, r_s, r_r, g_s, g_r, p_s, p_r, z_s, z_r, d_s, d_r, e_s, e_r,
):
    b, z = lax.axis_index("blk"), lax.axis_index("dp")
    core, px, py = b % 2, (b // 2) % 2, b // 4
    tokens, model = x_ref.shape
    block = wg_ref.shape[0]
    hidden = wg_ref.shape[1]
    per = 8 // dp
    weights = (wg_ref, wu_ref)
    tiles = [(lo, min(TILE, hidden - lo)) for lo in range(0, hidden, TILE)]

    def at(mask):
        return (
            b
            + (1 - 2 * core) * (mask % 2)
            + (2 - 4 * px) * ((mask // 2) % 2)
            + (4 - 8 * py) * (mask // 4)
        )

    def chip_start(mask):
        return at(mask) - core

    def remote(src, dst, send, recv, mask):
        return pltpu.make_async_remote_copy(
            src_ref=src, dst_ref=dst, send_sem=send, recv_sem=recv,
            device_id={"blk": at(mask)}, device_id_type=MESH,
        )

    def row_loop(body):
        def step(i, carry):
            body(pl.ds(pl.multiple_of(i * ROWS, ROWS), ROWS))
            return carry

        lax.fori_loop(0, tokens // ROWS, step, 0)

    barrier = pltpu.get_barrier_semaphore()
    for mask in range(1, 8):
        pl.semaphore_signal(barrier, inc=1, device_id={"blk": at(mask)}, device_id_type=MESH)
    for r in range(1, dp):
        pl.semaphore_signal(
            barrier, inc=1, device_id={"dp": (z + r) % dp}, device_id_type=MESH
        )

    def norm_rows(rows):
        wide = x_ref[rows, :].astype(jnp.float32)
        root = jnp.sqrt(jnp.mean(wide * wide, axis=1, keepdims=True) + 1e-05)
        rm[rows, :] = jnp.broadcast_to(root, (ROWS, 128))
        unit = wide / root
        for j in range(8):
            piece = unit[:, j * block : (j + 1) * block]
            un[j, rows, :] = piece
            nb[j, rows, :] = (piece * gain_ref[j]).astype(jnp.bfloat16)

    row_loop(norm_rows)
    pl.semaphore_wait(barrier, 7 + dp - 1)

    x_copies = {}
    for mask in (6, 7, 2, 3, 4, 5, 1):
        copy = remote(nb.at[at(mask)], xs.at[b], x_s.at[mask], x_r.at[mask], mask)
        copy.start()
        x_copies[mask] = copy
    xs[b] = nb[b]

    def columns(mask):
        return xs[pl.ds(chip_start(mask), 2)].reshape(2 * tokens, block)

    def x_arrived(mask):
        for m in (mask, mask + 1):
            if m:
                remote(nb.at[b], xs.at[at(m)], x_s.at[m], x_r.at[m], m).wait_recv()

    slot = {DIAG: 0, ACROSS_X: 1, ACROSS_Y: 2, OWN: 3}
    c_copies = {}

    def forward(mask, mat):
        k = slot[mask]
        lhs = columns(mask)
        for lo, width in tiles:
            out = jnp.dot(
                lhs, weights[mat][:, lo : lo + width], preferred_element_type=jnp.float32
            )
            pb[k, mat, :, :, lo : lo + width] = out.astype(jnp.bfloat16).reshape(
                2, tokens, width
            )
        copy = remote(pb.at[k, mat, 1 - core], rc.at[k, mat], c_s.at[k, mat], c_r.at[k, mat], 1)
        copy.start()
        c_copies[k, mat] = copy

    r_copies = {}

    def send_sum(mask, mat, e, to, extra=None):
        k = slot[mask]
        c_copies[k, mat].wait_recv()
        if extra is not None:
            r_copies[mat, extra].wait_recv()

        def rows_sum(rows):
            total = pb[k, mat, core, rows, :].astype(jnp.float32) + rc[k, mat, rows, :].astype(
                jnp.float32
            )
            if extra is not None:
                total = total + rbuf[mat, extra, rows, :].astype(jnp.float32)
            sbuf[mat, e, rows, :] = total.astype(jnp.bfloat16)

        row_loop(rows_sum)
        copy = remote(sbuf.at[mat, e], rbuf.at[mat, e], r_s.at[mat, e], r_r.at[mat, e], to)
        copy.start()
        r_copies[mat, e] = copy

    x_arrived(DIAG)
    forward(DIAG, 0)
    forward(DIAG, 1)
    x_arrived(ACROSS_X)
    forward(ACROSS_X, 0)
    send_sum(DIAG, 0, 0, ACROSS_X)
    send_sum(DIAG, 1, 0, ACROSS_Y)
    x_arrived(ACROSS_Y)
    forward(ACROSS_Y, 1)
    send_sum(ACROSS_X, 0, 1, ACROSS_X)
    send_sum(ACROSS_Y, 1, 1, ACROSS_Y)
    forward(ACROSS_Y, 0)
    forward(ACROSS_X, 1)
    x_arrived(OWN)
    forward(OWN, 0)
    forward(OWN, 1)
    for mask in (OWN, ACROSS_X, ACROSS_Y, DIAG):
        xt[slot[mask]] = columns(mask).T
    send_sum(ACROSS_Y, 0, 2, ACROSS_Y, extra=0)
    send_sum(ACROSS_X, 1, 2, ACROSS_X, extra=0)
    for mat in (0, 1):
        c_copies[3, mat].wait_recv()
        r_copies[mat, 1].wait_recv()
        r_copies[mat, 2].wait_recv()

    def act_rows(rows):
        pre = []
        for mat in (0, 1):
            total = pb[3, mat, core, rows, :].astype(jnp.float32) + rc[3, mat, rows, :].astype(
                jnp.float32
            )
            total = total + rbuf[mat, 1, rows, :].astype(jnp.float32)
            pre.append(total + rbuf[mat, 2, rows, :].astype(jnp.float32))
        gate_pre, up_pre = pre
        sig = jax.nn.sigmoid(gate_pre)
        activated = gate_pre * sig
        hid_ref[rows, :] = (activated * up_pre).astype(jnp.bfloat16)
        wide = up_ref[rows, :].astype(jnp.float32)
        full[1, b, rows, :] = (wide * activated).astype(jnp.bfloat16)
        full[0, b, rows, :] = (
            wide * up_pre * sig * (1.0 + gate_pre * (1.0 - sig))
        ).astype(jnp.bfloat16)

    row_loop(act_rows)

    g_sends = []

    def pass_on(mat, origin, to):
        there = origin ^ to
        t = at(origin)
        copy = remote(
            full.at[mat, t], full.at[mat, t], g_s.at[mat, there], g_r.at[mat, there], to
        )
        copy.start()
        g_sends.append(copy)

    def arrived(mat, origin):
        t = at(origin)
        remote(
            full.at[mat, t], full.at[mat, t], g_s.at[mat, origin], g_r.at[mat, origin], 1
        ).wait_recv()

    pass_on(0, OWN, ACROSS_X)
    pass_on(1, OWN, ACROSS_Y)
    pass_on(0, OWN, 1)
    pass_on(1, OWN, 1)
    pass_on(1, OWN, ACROSS_X)
    pass_on(0, OWN, ACROSS_Y)

    p_copies = {}

    def back(mask, first):
        k = slot[mask]
        start = chip_start(mask)
        grads = []
        for mat, out_ref in ((0, gg_ref), (1, gu_ref)):
            for lo, width in tiles:
                piece = full[mat, pl.ds(start, 2), :, lo : lo + width].reshape(2 * tokens, width)
                term = jnp.dot(xt[k], piece, preferred_element_type=jnp.float32)
                if first:
                    out_ref[:, lo : lo + width] = term
                else:
                    out_ref[:, lo : lo + width] += term
            grads.append(
                lax.dot_general(
                    full[mat, pl.ds(start, 2)].reshape(2 * tokens, hidden),
                    weights[mat][...],
                    (((1,), (1,)), ((), ())),
                    preferred_element_type=jnp.float32,
                )
            )
        ps[pl.ds(start, 2)] = (grads[0] + grads[1]).astype(jnp.bfloat16).reshape(2, tokens, block)
        for m in (mask, mask + 1):
            if m:
                copy = remote(ps.at[at(m)], pr.at[b], p_s.at[m], p_r.at[m], m)
                copy.start()
                p_copies[m] = copy
            else:
                pr[b] = ps[b]

    arrived(0, 1)
    arrived(1, 1)
    back(OWN, True)
    arrived(0, ACROSS_X)
    pass_on(0, ACROSS_X, ACROSS_Y)
    pass_on(0, ACROSS_X, 1)
    arrived(1, ACROSS_Y)
    pass_on(1, ACROSS_Y, ACROSS_X)
    pass_on(1, ACROSS_Y, 1)
    arrived(1, ACROSS_X)
    pass_on(1, ACROSS_X, 1)
    arrived(0, ACROSS_Y)
    pass_on(0, ACROSS_Y, 1)
    arrived(0, ACROSS_X + 1)
    arrived(1, ACROSS_X + 1)
    back(ACROSS_X, False)
    arrived(0, ACROSS_Y + 1)
    arrived(1, ACROSS_Y + 1)
    back(ACROSS_Y, False)
    arrived(0, DIAG)
    pass_on(0, DIAG, 1)
    arrived(1, DIAG)
    pass_on(1, DIAG, 1)
    arrived(0, DIAG + 1)
    arrived(1, DIAG + 1)
    back(DIAG, False)

    for m in range(1, 8):
        remote(ps.at[b], pr.at[at(m)], p_s.at[m], p_r.at[m], m).wait_recv()

    def over_dp(src, dst, send, recv, r):
        return pltpu.make_async_remote_copy(
            src_ref=src, dst_ref=dst, send_sem=send, recv_sem=recv,
            device_id={"dp": (z + r) % dp}, device_id_type=MESH,
        )

    z_copies = []
    for r in range(1, dp):
        to = (z + r) % dp
        copy = over_dp(pr.at[pl.ds(to * per, per)], zr.at[z], z_s.at[r], z_r.at[r], r)
        copy.start()
        z_copies.append(copy)

    dot = jnp.zeros((tokens, 1), jnp.float32)
    for j in range(8):
        dot = dot + jnp.sum(
            pr[j].astype(jnp.float32) * gain_ref[j] * un[j], axis=1, keepdims=True
        )
    dots[...] = jnp.broadcast_to(dot, (tokens, tokens)).T[0:8, :]
    for r in range(1, dp):
        copy = over_dp(dots, dotr.at[z], d_s.at[r], d_r.at[r], r)
        copy.start()
        z_copies.append(copy)
    for r in range(1, dp):
        source = (z + dp - r) % dp
        over_dp(pr.at[pl.ds(0, per)], zr.at[source], z_s.at[r], z_r.at[r], r).wait_recv()
    sums = []
    for jj in range(per):
        j = z * per + jj
        total = pr[j].astype(jnp.float32)
        for r in range(1, dp):
            total = total + zr[(z + r) % dp, jj].astype(jnp.float32)
        sums.append(total)
        part = jnp.sum(total * un[j], axis=0, keepdims=True)
        gsend[:, jj, :] = jnp.broadcast_to(part, (8, block))
    e_copies = []
    for m in range(1, 8):
        copy = remote(gsend, gsum.at[b], e_s.at[m], e_r.at[m], m)
        copy.start()
        e_copies.append(copy)
    total_dot = dots[...]
    for r in range(1, dp):
        source = (z + dp - r) % dp
        over_dp(dots, dotr.at[source], d_s.at[r], d_r.at[r], r).wait_recv()
        total_dot = total_dot + dotr[source]
    means = jnp.broadcast_to(total_dot[0:1, :] / model, (tokens, tokens)).T[:, 0:1]
    root = rm[:, 0:1]
    for jj in range(per):
        j = z * per + jj
        value = (sums[jj] * gain_ref[j] - un[j] * means) / root
        gi_ref[:, jj * block : (jj + 1) * block] = value.astype(jnp.bfloat16)
    total_gain = gsend[...]
    for m in range(1, 8):
        remote(gsend, gsum.at[at(m)], e_s.at[m], e_r.at[m], m).wait_recv()
        total_gain = total_gain + gsum[at(m)]
    ggain_ref[...] = total_gain[0]

    for group in (x_copies, c_copies, r_copies, p_copies):
        for copy in group.values():
            copy.wait_send()
    for copy in g_sends + z_copies + e_copies:
        copy.wait_send()


def by_kernel(dp, inputs, gain, w_gate, w_up, upstream):
    tokens, model = inputs.shape
    block, hidden = w_gate.shape
    per = 8 // dp
    bf16, f32 = jnp.bfloat16, jnp.float32
    vmem = pl.BlockSpec(memory_space=pltpu.VMEM)

    def dma(*shape):
        return pltpu.SemaphoreType.DMA(shape)

    hid, grad_gate, grad_up, grad_input, grad_gain = pl.pallas_call(
        functools.partial(plane_kernel, dp),
        out_shape=(
            jax.ShapeDtypeStruct((tokens, hidden), bf16),
            jax.ShapeDtypeStruct((block, hidden), f32),
            jax.ShapeDtypeStruct((block, hidden), f32),
            jax.ShapeDtypeStruct((tokens, per * block), bf16),
            jax.ShapeDtypeStruct((per, block), f32),
        ),
        in_specs=[vmem] * 5,
        out_specs=(vmem,) * 5,
        scratch_shapes=[
            pltpu.VMEM((8, tokens, block), bf16),
            pltpu.VMEM((8, tokens, block), f32),
            pltpu.VMEM((tokens, 128), f32),
            pltpu.VMEM((8, tokens, block), bf16),
            pltpu.VMEM((4, block, 2 * tokens), bf16),
            pltpu.VMEM((4, 2, 2, tokens, hidden), bf16),
            pltpu.VMEM((4, 2, tokens, hidden), bf16),
            pltpu.VMEM((2, 3, tokens, hidden), bf16),
            pltpu.VMEM((2, 3, tokens, hidden), bf16),
            pltpu.VMEM((2, 8, tokens, hidden), bf16),
            pltpu.VMEM((8, tokens, block), bf16),
            pltpu.VMEM((8, tokens, block), bf16),
            pltpu.VMEM((dp, per, tokens, block), bf16),
            pltpu.VMEM((8, tokens), f32),
            pltpu.VMEM((dp, 8, tokens), f32),
            pltpu.VMEM((8, 8, per, block), f32),
            pltpu.VMEM((8, per, block), f32),
            dma(8), dma(8), dma(4, 2), dma(4, 2), dma(2, 3), dma(2, 3), dma(2, 8), dma(2, 8),
            dma(8), dma(8), dma(dp), dma(dp), dma(dp), dma(dp), dma(8), dma(8),
        ],
        compiler_params=pltpu.CompilerParams(
            collective_id=0, has_side_effects=True, vmem_limit_bytes=60 * 2**20
        ),
        cost_estimate=pl.CostEstimate(
            flops=48 * tokens * block * hidden * 2,
            bytes_accessed=16 * block * hidden,
            transcendentals=tokens * hidden,
        ),
    )(inputs, gain.reshape(8, 1, block), w_gate, w_up, upstream)
    return hid, grad_gate, grad_up, grad_input, grad_gain.reshape(per * block)


def by_collectives(inputs, gain, w_gate, w_up, upstream):
    wide_input = inputs.astype(jnp.float32)
    root_mean = jnp.sqrt(jnp.mean(wide_input * wide_input, axis=1, keepdims=True) + 1e-05)
    unit_input = wide_input / root_mean
    normed = (unit_input * gain).astype(jnp.bfloat16)
    columns = lax.all_to_all(normed, "blk", split_axis=1, concat_axis=0, tiled=True)
    gate_part = jnp.dot(columns, w_gate, preferred_element_type=jnp.float32).astype(jnp.bfloat16)
    up_part = jnp.dot(columns, w_up, preferred_element_type=jnp.float32).astype(jnp.bfloat16)
    gate_pre = lax.psum_scatter(gate_part, "blk", scatter_dimension=0, tiled=True).astype(jnp.float32)
    up_pre = lax.psum_scatter(up_part, "blk", scatter_dimension=0, tiled=True).astype(jnp.float32)
    sigmoid_gate = jax.nn.sigmoid(gate_pre)
    activated = gate_pre * sigmoid_gate
    hidden = (activated * up_pre).astype(jnp.bfloat16)
    upstream_wide = upstream.astype(jnp.float32)
    back_up = (upstream_wide * activated).astype(jnp.bfloat16)
    back_gate = (
        upstream_wide * up_pre * sigmoid_gate * (1.0 + gate_pre * (1.0 - sigmoid_gate))
    ).astype(jnp.bfloat16)
    all_up = lax.all_gather(back_up, "blk", axis=0, tiled=True)
    all_gate = lax.all_gather(back_gate, "blk", axis=0, tiled=True)
    over_tokens = (((0,), (0,)), ((), ()))
    over_hidden = (((1,), (1,)), ((), ()))
    grad_up = lax.dot_general(columns, all_up, over_tokens, preferred_element_type=jnp.float32)
    grad_gate = lax.dot_general(columns, all_gate, over_tokens, preferred_element_type=jnp.float32)
    part = lax.dot_general(
        all_gate, w_gate, over_hidden, preferred_element_type=jnp.float32
    ) + lax.dot_general(all_up, w_up, over_hidden, preferred_element_type=jnp.float32)
    part = lax.all_to_all(
        part.astype(jnp.bfloat16), "blk", split_axis=0, concat_axis=1, tiled=True
    )
    feature_count = inputs.shape[1] // lax.axis_size("dp")
    feature_start = lax.axis_index("dp") * feature_count
    gain_slice = lax.dynamic_slice_in_dim(gain, feature_start, feature_count, 0)
    unit_slice = lax.dynamic_slice_in_dim(unit_input, feature_start, feature_count, 1)
    own_sums = lax.psum_scatter(part, "dp", scatter_dimension=1, tiled=True).astype(jnp.float32)
    token_totals = lax.psum(jnp.sum(own_sums * gain_slice * unit_slice, axis=1), "dp")
    token_means = token_totals[:, None] / inputs.shape[1]
    grad_input = ((own_sums * gain_slice - unit_slice * token_means) / root_mean).astype(
        jnp.bfloat16
    )
    grad_gain = lax.psum(jnp.sum(own_sums * unit_slice, axis=0), "blk")
    return (hidden, grad_gate, grad_up, grad_input, grad_gain)


def solution(mesh):
    dp = mesh.shape["dp"]
    by_chip = mesh.shape["blk"] == 8 and 8 % dp == 0
    return jax.shard_map(
        functools.partial(by_kernel, dp) if by_chip else by_collectives,
        mesh=mesh,
        in_specs=(P("blk", None), P(), P("blk", "dp"), P("blk", "dp"), P("blk", "dp")),
        out_specs=(P("blk", "dp"), P("blk", "dp"), P("blk", "dp"), P("blk", "dp"), P("dp")),
        check_vma=False,
    )
```

```python
import functools

import jax
import jax.numpy as jnp
from jax import lax
from jax.experimental import pallas as pl
from jax.experimental.pallas import tpu as pltpu
from jax.sharding import PartitionSpec as P

MESH = pl.DeviceIdType.MESH
ROWS = 16
TILE = 256
DIAG, ACROSS_X, ACROSS_Y, OWN = 6, 2, 4, 0
SLOT = {DIAG: 0, ACROSS_X: 1, ACROSS_Y: 2, OWN: 3}


def chunks_of(hidden):
    first = (hidden // TILE + 2) // 2 * TILE
    return ((0, first), (first, hidden - first))


def plane_kernel(
    dp, x_ref, gain_ref, wg_ref, wu_ref, up_ref,
    hid_ref, gg_ref, gu_ref, gi_ref, ggain_ref,
    nb, un, gs, rm, xs, xt, wgs, wus, ggs, gus, hid, pacc, ps, pr, zr, dots, dotr, gsum, gsend,
    ups0, hs0, pb0, rc0, sbuf0, rbuf0, full0,
    ups1, hs1, pb1, rc1, sbuf1, rbuf1, full1,
    x_s, x_r, c_s, c_r, r_s, r_r, g_s, g_r, p_s, p_r, z_s, z_r, d_s, d_r, e_s, e_r, l_s,
):
    b, z = lax.axis_index("blk"), lax.axis_index("dp")
    core, px, py = b % 2, (b // 2) % 2, b // 4
    tokens, model = x_ref.shape
    block, hidden = wgs.shape
    per = 8 // dp
    weights = (wgs, wus)
    chunks = chunks_of(hidden)
    ups, hs, pb, rc = (ups0, ups1), (hs0, hs1), (pb0, pb1), (rc0, rc1)
    sbuf, rbuf, full = (sbuf0, sbuf1), (rbuf0, rbuf1), (full0, full1)

    def tiles(h):
        width = chunks[h][1]
        return [(lo, min(TILE, width - lo)) for lo in range(0, width, TILE)]

    def at(mask):
        return (
            b
            + (1 - 2 * core) * (mask % 2)
            + (2 - 4 * px) * ((mask // 2) % 2)
            + (4 - 8 * py) * (mask // 4)
        )

    def chip_start(mask):
        return at(mask) - core

    def remote(src, dst, send, recv, mask):
        return pltpu.make_async_remote_copy(
            src_ref=src, dst_ref=dst, send_sem=send, recv_sem=recv,
            device_id={"blk": at(mask)}, device_id_type=MESH,
        )

    def over_dp(src, dst, send, recv, to):
        return pltpu.make_async_remote_copy(
            src_ref=src, dst_ref=dst, send_sem=send, recv_sem=recv,
            device_id={"dp": to}, device_id_type=MESH,
        )

    def row_loop(body):
        def step(i, carry):
            body(pl.ds(pl.multiple_of(i * ROWS, ROWS), ROWS))
            return carry

        lax.fori_loop(0, tokens // ROWS, step, 0)

    barrier = pltpu.get_barrier_semaphore()
    for mask in range(1, 8):
        pl.semaphore_signal(barrier, inc=1, device_id={"blk": at(mask)}, device_id_type=MESH)
    for r in range(1, dp):
        pl.semaphore_signal(
            barrier, inc=1, device_id={"dp": (z + r) % dp}, device_id_type=MESH
        )
    loads = [
        pltpu.make_async_copy(wg_ref, wgs, l_s.at[0]),
        pltpu.make_async_copy(wu_ref, wus, l_s.at[1]),
    ]
    for copy in loads:
        copy.start()
    for j in range(8):
        gs[j] = gain_ref[:, j * block : (j + 1) * block]

    def norm_rows(rows):
        wide = x_ref[rows, :].astype(jnp.float32)
        root = jnp.sqrt(jnp.mean(wide * wide, axis=1, keepdims=True) + 1e-05)
        rm[rows, :] = jnp.broadcast_to(root, (ROWS, 128))
        unit = wide / root
        for j in range(8):
            piece = unit[:, j * block : (j + 1) * block]
            un[j, rows, :] = piece
            nb[j, rows, :] = (piece * gs[j]).astype(jnp.bfloat16)

    row_loop(norm_rows)
    pl.semaphore_wait(barrier, 7 + dp - 1)

    sends = []

    def start(copy):
        copy.start()
        sends.append(copy)
        return copy

    for mask in (6, 7, 2, 3, 4, 5, 1):
        start(remote(nb.at[at(mask)], xs.at[b], x_s.at[mask], x_r.at[mask], mask))
    xs[b] = nb[b]
    for copy in loads:
        copy.wait()

    def columns(mask):
        return xs[pl.ds(chip_start(mask), 2)].reshape(2 * tokens, block)

    def x_arrived(mask):
        for m in (mask, mask + 1):
            if m:
                remote(nb.at[b], xs.at[at(m)], x_s.at[m], x_r.at[m], m).wait_recv()

    c_copies, r_copies = {}, {}

    def forward(mask, mat, h):
        k = SLOT[mask]
        lhs = columns(mask)
        base = chunks[h][0]
        for lo, width in tiles(h):
            out = jnp.dot(
                lhs,
                weights[mat][:, base + lo : base + lo + width],
                preferred_element_type=jnp.float32,
            )
            pb[h][k, mat, :, :, lo : lo + width] = out.astype(jnp.bfloat16).reshape(
                2, tokens, width
            )
        c_copies[k, mat, h] = start(
            remote(
                pb[h].at[k, mat, 1 - core], rc[h].at[k, mat],
                c_s.at[h, k, mat], c_r.at[h, k, mat], 1,
            )
        )

    def send_sum(mask, mat, e, to, h, extra=None):
        k = SLOT[mask]
        c_copies[k, mat, h].wait_recv()
        if extra is not None:
            r_copies[mat, extra, h].wait_recv()

        def rows_sum(rows):
            total = pb[h][k, mat, core, rows, :].astype(jnp.float32)
            total = total + rc[h][k, mat, rows, :].astype(jnp.float32)
            if extra is not None:
                total = total + rbuf[h][mat, extra, rows, :].astype(jnp.float32)
            sbuf[h][mat, e, rows, :] = total.astype(jnp.bfloat16)

        row_loop(rows_sum)
        r_copies[mat, e, h] = start(
            remote(
                sbuf[h].at[mat, e], rbuf[h].at[mat, e],
                r_s.at[h, mat, e], r_r.at[h, mat, e], to,
            )
        )

    def activate(h):
        for mat in (0, 1):
            c_copies[3, mat, h].wait_recv()
            r_copies[mat, 1, h].wait_recv()
            r_copies[mat, 2, h].wait_recv()

        def act_rows(rows):
            pre = []
            for mat in (0, 1):
                total = pb[h][3, mat, core, rows, :].astype(jnp.float32)
                total = total + rc[h][3, mat, rows, :].astype(jnp.float32)
                total = total + rbuf[h][mat, 1, rows, :].astype(jnp.float32)
                pre.append(total + rbuf[h][mat, 2, rows, :].astype(jnp.float32))
            gate_pre, up_pre = pre
            sig = jax.nn.sigmoid(gate_pre)
            activated = gate_pre * sig
            hs[h][rows, :] = (activated * up_pre).astype(jnp.bfloat16)
            wide = ups[h][rows, :].astype(jnp.float32)
            full[h][1, b, rows, :] = (wide * activated).astype(jnp.bfloat16)
            full[h][0, b, rows, :] = (
                wide * up_pre * sig * (1.0 + gate_pre * (1.0 - sig))
            ).astype(jnp.bfloat16)

        row_loop(act_rows)
        pass_on(0, OWN, ACROSS_X, h)
        pass_on(1, OWN, ACROSS_Y, h)
        pass_on(0, OWN, 1, h)
        pass_on(1, OWN, 1, h)
        pass_on(1, OWN, ACROSS_X, h)
        pass_on(0, OWN, ACROSS_Y, h)

    def pass_on(mat, origin, to, h):
        there = origin ^ to
        t = at(origin)
        start(
            remote(
                full[h].at[mat, t], full[h].at[mat, t],
                g_s.at[h, mat, there], g_r.at[h, mat, there], to,
            )
        )

    def arrived(mat, origin, h):
        t = at(origin)
        remote(
            full[h].at[mat, t], full[h].at[mat, t],
            g_s.at[h, mat, origin], g_r.at[h, mat, origin], 1,
        ).wait_recv()

    def back_inputs(mask, h):
        base, width = chunks[h]
        first = chip_start(mask)
        part = pacc[SLOT[mask]] if h else None
        for mat in (0, 1):
            term = lax.dot_general(
                full[h][mat, pl.ds(first, 2)].reshape(2 * tokens, width),
                weights[mat][:, base : base + width],
                (((1,), (1,)), ((), ())),
                preferred_element_type=jnp.float32,
            )
            part = term if part is None else part + term
        if h == 0:
            pacc[SLOT[mask]] = part
            return
        ps[pl.ds(first, 2)] = part.astype(jnp.bfloat16).reshape(2, tokens, block)
        for m in (mask, mask + 1):
            if m:
                start(remote(ps.at[at(m)], pr.at[b], p_s.at[m], p_r.at[m], m))
            else:
                pr[b] = ps[b]

    def back_weights(mask, h):
        base = chunks[h][0]
        for mat, out_ref in ((0, ggs), (1, gus)):
            for lo, width in tiles(h):
                piece = full[h][mat, pl.ds(chip_start(mask), 2), :, lo : lo + width]
                term = jnp.dot(
                    xt[SLOT[mask]],
                    piece.reshape(2 * tokens, width),
                    preferred_element_type=jnp.float32,
                )
                if mask == OWN:
                    out_ref[:, base + lo : base + lo + width] = term
                else:
                    out_ref[:, base + lo : base + lo + width] += term

    def forward_first(h):
        arrived(0, ACROSS_X, h)
        pass_on(0, ACROSS_X, ACROSS_Y, h)
        pass_on(0, ACROSS_X, 1, h)
        arrived(1, ACROSS_Y, h)
        pass_on(1, ACROSS_Y, ACROSS_X, h)
        pass_on(1, ACROSS_Y, 1, h)

    def forward_second(h):
        arrived(1, ACROSS_X, h)
        pass_on(1, ACROSS_X, 1, h)
        arrived(0, ACROSS_Y, h)
        pass_on(0, ACROSS_Y, 1, h)

    def forward_last(h):
        arrived(1, DIAG, h)
        pass_on(1, DIAG, 1, h)
        arrived(0, DIAG, h)
        pass_on(0, DIAG, 1, h)

    def other_core(mask, h):
        arrived(0, mask + 1, h)
        arrived(1, mask + 1, h)

    x_arrived(DIAG)
    forward(DIAG, 0, 0)
    forward(DIAG, 1, 0)
    x_arrived(ACROSS_X)
    forward(ACROSS_X, 0, 0)
    send_sum(DIAG, 0, 0, ACROSS_X, 0)
    send_sum(DIAG, 1, 0, ACROSS_Y, 0)
    x_arrived(ACROSS_Y)
    forward(ACROSS_Y, 1, 0)
    send_sum(ACROSS_X, 0, 1, ACROSS_X, 0)
    send_sum(ACROSS_Y, 1, 1, ACROSS_Y, 0)
    forward(ACROSS_Y, 0, 0)
    forward(ACROSS_X, 1, 0)
    x_arrived(OWN)
    forward(OWN, 0, 0)
    forward(OWN, 1, 0)
    forward(DIAG, 0, 1)
    forward(DIAG, 1, 1)
    for h, (base, width) in enumerate(chunks):
        ups[h][...] = up_ref[base : base + width, :].T
    send_sum(ACROSS_Y, 0, 2, ACROSS_Y, 0, extra=0)
    send_sum(ACROSS_X, 1, 2, ACROSS_X, 0, extra=0)
    send_sum(DIAG, 0, 0, ACROSS_X, 1)
    send_sum(DIAG, 1, 0, ACROSS_Y, 1)
    forward(ACROSS_X, 0, 1)
    forward(ACROSS_Y, 1, 1)
    forward(ACROSS_Y, 0, 1)
    forward(ACROSS_X, 1, 1)
    send_sum(ACROSS_X, 0, 1, ACROSS_X, 1)
    send_sum(ACROSS_Y, 1, 1, ACROSS_Y, 1)
    forward(OWN, 0, 1)
    forward(OWN, 1, 1)
    for mask in (OWN, ACROSS_X, ACROSS_Y, DIAG):
        xt[SLOT[mask]] = columns(mask).T
    activate(0)
    send_sum(ACROSS_Y, 0, 2, ACROSS_Y, 1, extra=0)
    send_sum(ACROSS_X, 1, 2, ACROSS_X, 1, extra=0)
    hid[0 : chunks[0][1], :] = hs[0][...].T
    forward_first(0)
    activate(1)
    other_core(OWN, 0)
    back_inputs(OWN, 0)
    back_weights(OWN, 0)
    forward_second(0)
    other_core(ACROSS_X, 0)
    back_inputs(ACROSS_X, 0)
    other_core(ACROSS_Y, 0)
    back_inputs(ACROSS_Y, 0)
    forward_last(0)
    hid[chunks[1][0] : hidden, :] = hs[1][...].T
    stores = [pltpu.make_async_copy(hid, hid_ref, l_s.at[2])]
    stores[0].start()
    back_weights(ACROSS_X, 0)
    forward_first(1)
    back_weights(ACROSS_Y, 0)
    other_core(DIAG, 0)
    back_inputs(DIAG, 0)
    other_core(OWN, 1)
    back_inputs(OWN, 1)
    forward_second(1)
    back_weights(DIAG, 0)

    dot = [jnp.zeros((tokens, 1), jnp.float32)]

    def collect(mask):
        for m in (mask, mask + 1):
            if m:
                remote(ps.at[b], pr.at[at(m)], p_s.at[m], p_r.at[m], m).wait_recv()
        first = chip_start(mask)
        to = first // per

        @pl.when(to != z)
        def _():
            r = (to - z + dp) % dp
            over_dp(pr.at[pl.ds(first, per)], zr.at[z], z_s.at[r], z_r.at[r], to).start()

        for c in range(2):
            j = first + c
            dot[0] = dot[0] + jnp.sum(
                pr[j].astype(jnp.float32) * gs[j] * un[j], axis=1, keepdims=True
            )

    other_core(ACROSS_X, 1)
    back_inputs(ACROSS_X, 1)
    other_core(ACROSS_Y, 1)
    back_inputs(ACROSS_Y, 1)
    back_weights(OWN, 1)
    collect(OWN)
    forward_last(1)
    back_weights(ACROSS_X, 1)
    other_core(DIAG, 1)
    back_inputs(DIAG, 1)
    collect(ACROSS_X)
    collect(ACROSS_Y)
    back_weights(ACROSS_Y, 1)
    collect(DIAG)
    dots[...] = jnp.broadcast_to(dot[0], (tokens, tokens)).T[0:8, :]
    for r in range(1, dp):
        start(over_dp(dots, dotr.at[z], d_s.at[r], d_r.at[r], (z + r) % dp))
    back_weights(DIAG, 1)
    for i, (held, out_ref) in enumerate(((ggs, gg_ref), (gus, gu_ref))):
        copy = pltpu.make_async_copy(held, out_ref, l_s.at[3 + i])
        copy.start()
        stores.append(copy)

    for r in range(1, dp):
        source = (z + dp - r) % dp
        over_dp(
            pr.at[pl.ds(0, per)], zr.at[source], z_s.at[r], z_r.at[r], source
        ).wait_recv()
    sums = []
    for jj in range(per):
        j = z * per + jj
        total = pr[j].astype(jnp.float32)
        for r in range(1, dp):
            total = total + zr[(z + r) % dp, jj].astype(jnp.float32)
        sums.append(total)
        part = jnp.sum(total * un[j], axis=0, keepdims=True)
        gsend[jj] = jnp.broadcast_to(part, (8, block))
    for m in range(1, 8):
        start(remote(gsend, gsum.at[b], e_s.at[m], e_r.at[m], m))
    total_dot = dots[...]
    for r in range(1, dp):
        source = (z + dp - r) % dp
        over_dp(dots, dotr.at[source], d_s.at[r], d_r.at[r], source).wait_recv()
        total_dot = total_dot + dotr[source]
    means = jnp.broadcast_to(total_dot[0:1, :] / model, (tokens, tokens)).T[:, 0:1]
    root = rm[:, 0:1]
    for jj in range(per):
        j = z * per + jj
        value = (sums[jj] * gs[j] - un[j] * means) / root
        gi_ref[:, jj * block : (jj + 1) * block] = value.astype(jnp.bfloat16)
    total_gain = gsend[...]
    for m in range(1, 8):
        remote(gsend, gsum.at[at(m)], e_s.at[m], e_r.at[m], m).wait_recv()
        total_gain = total_gain + gsum[at(m)]
    for jj in range(per):
        ggain_ref[:, jj * block : (jj + 1) * block] = total_gain[jj, 0:1, :]

    for copy in sends:
        copy.wait_send()
    for r in range(1, dp):
        over_dp(pr.at[pl.ds(0, per)], zr.at[z], z_s.at[r], z_r.at[r], (z + r) % dp).wait_send()
    for copy in stores:
        copy.wait()


def by_kernel(dp, inputs, gain, w_gate, w_up, upstream):
    tokens, model = inputs.shape
    block, hidden = w_gate.shape
    per = 8 // dp
    bf16, f32 = jnp.bfloat16, jnp.float32
    vmem = pl.BlockSpec(memory_space=pltpu.VMEM)
    hbm = pl.BlockSpec(memory_space=pl.ANY)

    def dma(*shape):
        return pltpu.SemaphoreType.DMA(shape)

    by_chunk = []
    for _, width in chunks_of(hidden):
        by_chunk += [
            pltpu.VMEM((tokens, width), bf16),
            pltpu.VMEM((tokens, width), bf16),
            pltpu.VMEM((4, 2, 2, tokens, width), bf16),
            pltpu.VMEM((4, 2, tokens, width), bf16),
            pltpu.VMEM((2, 3, tokens, width), bf16),
            pltpu.VMEM((2, 3, tokens, width), bf16),
            pltpu.VMEM((2, 8, tokens, width), bf16),
        ]
    hid, grad_gate, grad_up, grad_input, grad_gain = pl.pallas_call(
        functools.partial(plane_kernel, dp),
        out_shape=(
            jax.ShapeDtypeStruct((hidden, tokens), bf16),
            jax.ShapeDtypeStruct((block, hidden), f32),
            jax.ShapeDtypeStruct((block, hidden), f32),
            jax.ShapeDtypeStruct((tokens, per * block), bf16),
            jax.ShapeDtypeStruct((1, per * block), f32),
        ),
        in_specs=[vmem, vmem, hbm, hbm, vmem],
        out_specs=(hbm, hbm, hbm, vmem, vmem),
        scratch_shapes=[
            pltpu.VMEM((8, tokens, block), bf16),
            pltpu.VMEM((8, tokens, block), f32),
            pltpu.VMEM((8, 1, block), f32),
            pltpu.VMEM((tokens, 128), f32),
            pltpu.VMEM((8, tokens, block), bf16),
            pltpu.VMEM((4, block, 2 * tokens), bf16),
            pltpu.VMEM((block, hidden), bf16),
            pltpu.VMEM((block, hidden), bf16),
            pltpu.VMEM((block, hidden), f32),
            pltpu.VMEM((block, hidden), f32),
            pltpu.VMEM((hidden, tokens), bf16),
            pltpu.VMEM((4, 2 * tokens, block), f32),
            pltpu.VMEM((8, tokens, block), bf16),
            pltpu.VMEM((8, tokens, block), bf16),
            pltpu.VMEM((dp, per, tokens, block), bf16),
            pltpu.VMEM((8, tokens), f32),
            pltpu.VMEM((dp, 8, tokens), f32),
            pltpu.VMEM((8, per, 8, block), f32),
            pltpu.VMEM((per, 8, block), f32),
            *by_chunk,
            dma(8), dma(8), dma(2, 4, 2), dma(2, 4, 2), dma(2, 2, 3), dma(2, 2, 3),
            dma(2, 2, 8), dma(2, 2, 8), dma(8), dma(8), dma(dp), dma(dp), dma(dp), dma(dp),
            dma(8), dma(8), dma(5),
        ],
        compiler_params=pltpu.CompilerParams(
            collective_id=0, has_side_effects=True, vmem_limit_bytes=60 * 2**20
        ),
        cost_estimate=pl.CostEstimate(
            flops=48 * tokens * block * hidden * 2,
            bytes_accessed=16 * block * hidden,
            transcendentals=tokens * hidden,
        ),
    )(inputs, gain.reshape(1, model), w_gate, w_up, upstream.T)
    return hid.T, grad_gate, grad_up, grad_input, grad_gain.reshape(per * block)


def by_collectives(inputs, gain, w_gate, w_up, upstream):
    wide_input = inputs.astype(jnp.float32)
    root_mean = jnp.sqrt(jnp.mean(wide_input * wide_input, axis=1, keepdims=True) + 1e-05)
    unit_input = wide_input / root_mean
    normed = (unit_input * gain).astype(jnp.bfloat16)
    columns = lax.all_to_all(normed, "blk", split_axis=1, concat_axis=0, tiled=True)
    gate_part = jnp.dot(columns, w_gate, preferred_element_type=jnp.float32).astype(jnp.bfloat16)
    up_part = jnp.dot(columns, w_up, preferred_element_type=jnp.float32).astype(jnp.bfloat16)
    gate_pre = lax.psum_scatter(gate_part, "blk", scatter_dimension=0, tiled=True).astype(jnp.float32)
    up_pre = lax.psum_scatter(up_part, "blk", scatter_dimension=0, tiled=True).astype(jnp.float32)
    sigmoid_gate = jax.nn.sigmoid(gate_pre)
    activated = gate_pre * sigmoid_gate
    hidden = (activated * up_pre).astype(jnp.bfloat16)
    upstream_wide = upstream.astype(jnp.float32)
    back_up = (upstream_wide * activated).astype(jnp.bfloat16)
    back_gate = (
        upstream_wide * up_pre * sigmoid_gate * (1.0 + gate_pre * (1.0 - sigmoid_gate))
    ).astype(jnp.bfloat16)
    all_up = lax.all_gather(back_up, "blk", axis=0, tiled=True)
    all_gate = lax.all_gather(back_gate, "blk", axis=0, tiled=True)
    over_tokens = (((0,), (0,)), ((), ()))
    over_hidden = (((1,), (1,)), ((), ()))
    grad_up = lax.dot_general(columns, all_up, over_tokens, preferred_element_type=jnp.float32)
    grad_gate = lax.dot_general(columns, all_gate, over_tokens, preferred_element_type=jnp.float32)
    part = lax.dot_general(
        all_gate, w_gate, over_hidden, preferred_element_type=jnp.float32
    ) + lax.dot_general(all_up, w_up, over_hidden, preferred_element_type=jnp.float32)
    part = lax.all_to_all(
        part.astype(jnp.bfloat16), "blk", split_axis=0, concat_axis=1, tiled=True
    )
    feature_count = inputs.shape[1] // lax.axis_size("dp")
    feature_start = lax.axis_index("dp") * feature_count
    gain_slice = lax.dynamic_slice_in_dim(gain, feature_start, feature_count, 0)
    unit_slice = lax.dynamic_slice_in_dim(unit_input, feature_start, feature_count, 1)
    own_sums = lax.psum_scatter(part, "dp", scatter_dimension=1, tiled=True).astype(jnp.float32)
    token_totals = lax.psum(jnp.sum(own_sums * gain_slice * unit_slice, axis=1), "dp")
    token_means = token_totals[:, None] / inputs.shape[1]
    grad_input = ((own_sums * gain_slice - unit_slice * token_means) / root_mean).astype(
        jnp.bfloat16
    )
    grad_gain = lax.psum(jnp.sum(own_sums * unit_slice, axis=0), "blk")
    return (hidden, grad_gate, grad_up, grad_input, grad_gain)


def solution(mesh):
    dp = mesh.shape["dp"]
    by_chip = mesh.shape["blk"] == 8 and dp == 4
    return jax.shard_map(
        functools.partial(by_kernel, dp) if by_chip else by_collectives,
        mesh=mesh,
        in_specs=(P("blk", None), P(), P("blk", "dp"), P("blk", "dp"), P("blk", "dp")),
        out_specs=(P("blk", "dp"), P("blk", "dp"), P("blk", "dp"), P("blk", "dp"), P("dp")),
        check_vma=False,
    )
```

```python
import functools

import jax
import jax.numpy as jnp
from jax import lax
from jax.experimental import pallas as pl
from jax.experimental.pallas import tpu as pltpu
from jax.sharding import PartitionSpec as P

MESH = pl.DeviceIdType.MESH
ROWS = 16
TILE = 256
DIAG, ACROSS_X, ACROSS_Y, OWN = 6, 2, 4, 0
SLOT = {DIAG: 0, ACROSS_X: 1, ACROSS_Y: 2, OWN: 3}


def chunks_of(hidden):
    first = (hidden // TILE + 2) // 2 * TILE
    return ((0, first), (first, hidden - first))


def plane_kernel(
    dp, x_ref, gain_ref, wg_ref, wu_ref, up_ref,
    hid_ref, gg_ref, gu_ref, gi_ref, ggain_ref,
    gain_row, nb, un, gs, rm, xs, xt, wgs, wus, ggs, gus, hid, pacc, ps, pr, zr, dots, dotr, gsum, gsend, gtot, gz,
    ups0, hs0, pb0, rc0, sbuf0, rbuf0, full0,
    ups1, hs1, pb1, rc1, sbuf1, rbuf1, full1,
    x_s, x_r, c_s, c_r, r_s, r_r, g_s, g_r, p_s, p_r, z_s, z_r, d_s, d_r, e_s, e_r, f_s, f_r, l_s,
):
    b, z = lax.axis_index("blk"), lax.axis_index("dp")
    core, px, py = b % 2, (b // 2) % 2, b // 4
    tokens, model = x_ref.shape
    block, hidden = wgs.shape
    per = 8 // dp
    weights = (wgs, wus)
    chunks = chunks_of(hidden)
    ups, hs, pb, rc = (ups0, ups1), (hs0, hs1), (pb0, pb1), (rc0, rc1)
    sbuf, rbuf, full = (sbuf0, sbuf1), (rbuf0, rbuf1), (full0, full1)

    def tiles(h):
        width = chunks[h][1]
        return [(lo, min(TILE, width - lo)) for lo in range(0, width, TILE)]

    def at(mask):
        return (
            b
            + (1 - 2 * core) * (mask % 2)
            + (2 - 4 * px) * ((mask // 2) % 2)
            + (4 - 8 * py) * (mask // 4)
        )

    def chip_start(mask):
        return at(mask) - core

    def remote(src, dst, send, recv, mask):
        return pltpu.make_async_remote_copy(
            src_ref=src, dst_ref=dst, send_sem=send, recv_sem=recv,
            device_id={"blk": at(mask)}, device_id_type=MESH,
        )

    def over_dp(src, dst, send, recv, to):
        return pltpu.make_async_remote_copy(
            src_ref=src, dst_ref=dst, send_sem=send, recv_sem=recv,
            device_id={"dp": to}, device_id_type=MESH,
        )

    def row_loop(body):
        def step(i, carry):
            body(pl.ds(pl.multiple_of(i * ROWS, ROWS), ROWS))
            return carry

        lax.fori_loop(0, tokens // ROWS, step, 0)

    barrier = pltpu.get_barrier_semaphore()
    for mask in range(1, 8):
        pl.semaphore_signal(barrier, inc=1, device_id={"blk": at(mask)}, device_id_type=MESH)
    for r in range(1, dp):
        pl.semaphore_signal(
            barrier, inc=1, device_id={"dp": (z + r) % dp}, device_id_type=MESH
        )
    loads = [
        pltpu.make_async_copy(wg_ref, wgs, l_s.at[0]),
        pltpu.make_async_copy(wu_ref, wus, l_s.at[1]),
    ]
    for copy in loads:
        copy.start()
    gain_load = pltpu.make_async_copy(gain_ref, gain_row.at[0], l_s.at[2])
    gain_load.start()
    gain_load.wait()
    for j in range(8):
        gs[j] = gain_row[:, j * block : (j + 1) * block]

    def norm_rows(rows):
        wide = x_ref[rows, :].astype(jnp.float32)
        root = jnp.sqrt(jnp.mean(wide * wide, axis=1, keepdims=True) + 1e-05)
        rm[rows, :] = jnp.broadcast_to(root, (ROWS, 128))
        unit = wide / root
        for j in range(8):
            piece = unit[:, j * block : (j + 1) * block]
            un[j, rows, :] = piece
            nb[j, rows, :] = (piece * gs[j]).astype(jnp.bfloat16)

    row_loop(norm_rows)
    pl.semaphore_wait(barrier, 7 + dp - 1)

    sends = []

    def start(copy):
        copy.start()
        sends.append(copy)
        return copy

    def send_normed(mask):
        copy = remote(nb.at[at(mask)], xs.at[b], x_s.at[mask], x_r.at[mask], mask)
        copy.start()
        return copy

    far = [send_normed(mask) for mask in (6, 7)]
    sends.append(send_normed(1))
    xs[b] = nb[b]
    for copy in far:
        copy.wait_send()
    sends.extend(send_normed(mask) for mask in (2, 4, 3, 5))
    for copy in loads:
        copy.wait()

    def columns(mask):
        return xs[pl.ds(chip_start(mask), 2)].reshape(2 * tokens, block)

    def x_arrived(mask):
        for m in (mask, mask + 1):
            if m:
                remote(nb.at[b], xs.at[at(m)], x_s.at[m], x_r.at[m], m).wait_recv()

    c_copies, r_copies = {}, {}

    def forward(mask, mat, h):
        k = SLOT[mask]
        lhs = columns(mask)
        base = chunks[h][0]
        for lo, width in tiles(h):
            out = jnp.dot(
                lhs,
                weights[mat][:, base + lo : base + lo + width],
                preferred_element_type=jnp.float32,
            )
            pb[h][k, mat, :, :, lo : lo + width] = out.astype(jnp.bfloat16).reshape(
                2, tokens, width
            )
        c_copies[k, mat, h] = start(
            remote(
                pb[h].at[k, mat, 1 - core], rc[h].at[k, mat],
                c_s.at[h, k, mat], c_r.at[h, k, mat], 1,
            )
        )

    def send_sum(mask, mat, e, to, h, extra=None):
        k = SLOT[mask]
        c_copies[k, mat, h].wait_recv()
        if extra is not None:
            r_copies[mat, extra, h].wait_recv()

        def rows_sum(rows):
            total = pb[h][k, mat, core, rows, :].astype(jnp.float32)
            total = total + rc[h][k, mat, rows, :].astype(jnp.float32)
            if extra is not None:
                total = total + rbuf[h][mat, extra, rows, :].astype(jnp.float32)
            sbuf[h][mat, e, rows, :] = total.astype(jnp.bfloat16)

        row_loop(rows_sum)
        r_copies[mat, e, h] = start(
            remote(
                sbuf[h].at[mat, e], rbuf[h].at[mat, e],
                r_s.at[h, mat, e], r_r.at[h, mat, e], to,
            )
        )

    def activate(h):
        for mat in (0, 1):
            c_copies[3, mat, h].wait_recv()
            r_copies[mat, 1, h].wait_recv()
            r_copies[mat, 2, h].wait_recv()

        def act_rows(rows):
            pre = []
            for mat in (0, 1):
                total = pb[h][3, mat, core, rows, :].astype(jnp.float32)
                total = total + rc[h][3, mat, rows, :].astype(jnp.float32)
                total = total + rbuf[h][mat, 1, rows, :].astype(jnp.float32)
                pre.append(total + rbuf[h][mat, 2, rows, :].astype(jnp.float32))
            gate_pre, up_pre = pre
            sig = jax.nn.sigmoid(gate_pre)
            activated = gate_pre * sig
            hs[h][rows, :] = (activated * up_pre).astype(jnp.bfloat16)
            wide = ups[h][rows, :].astype(jnp.float32)
            full[h][1, b, rows, :] = (wide * activated).astype(jnp.bfloat16)
            full[h][0, b, rows, :] = (
                wide * up_pre * sig * (1.0 + gate_pre * (1.0 - sig))
            ).astype(jnp.bfloat16)

        row_loop(act_rows)
        pass_on(0, OWN, ACROSS_X, h)
        pass_on(1, OWN, ACROSS_Y, h)
        pass_on(0, OWN, 1, h)
        pass_on(1, OWN, 1, h)
        pass_on(1, OWN, ACROSS_X, h)
        pass_on(0, OWN, ACROSS_Y, h)

    def pass_on(mat, origin, to, h):
        there = origin ^ to
        t = at(origin)
        start(
            remote(
                full[h].at[mat, t], full[h].at[mat, t],
                g_s.at[h, mat, there], g_r.at[h, mat, there], to,
            )
        )

    def arrived(mat, origin, h):
        t = at(origin)
        remote(
            full[h].at[mat, t], full[h].at[mat, t],
            g_s.at[h, mat, origin], g_r.at[h, mat, origin], 1,
        ).wait_recv()

    def back_inputs(mask, h):
        base, width = chunks[h]
        first = chip_start(mask)
        part = pacc[SLOT[mask]] if h else None
        for mat in (0, 1):
            term = lax.dot_general(
                full[h][mat, pl.ds(first, 2)].reshape(2 * tokens, width),
                weights[mat][:, base : base + width],
                (((1,), (1,)), ((), ())),
                preferred_element_type=jnp.float32,
            )
            part = term if part is None else part + term
        if h == 0:
            pacc[SLOT[mask]] = part
            return
        ps[pl.ds(first, 2)] = part.astype(jnp.bfloat16).reshape(2, tokens, block)
        for m in (mask, mask + 1):
            if m:
                start(remote(ps.at[at(m)], pr.at[b], p_s.at[m], p_r.at[m], m))
            else:
                pr[b] = ps[b]

    def back_weights(mask, h):
        base = chunks[h][0]
        for mat, out_ref in ((0, ggs), (1, gus)):
            for lo, width in tiles(h):
                piece = full[h][mat, pl.ds(chip_start(mask), 2), :, lo : lo + width]
                term = jnp.dot(
                    xt[SLOT[mask]],
                    piece.reshape(2 * tokens, width),
                    preferred_element_type=jnp.float32,
                )
                if mask == OWN:
                    out_ref[:, base + lo : base + lo + width] = term
                else:
                    out_ref[:, base + lo : base + lo + width] += term

    def forward_first(h):
        arrived(0, ACROSS_X, h)
        pass_on(0, ACROSS_X, ACROSS_Y, h)
        pass_on(0, ACROSS_X, 1, h)
        arrived(1, ACROSS_Y, h)
        pass_on(1, ACROSS_Y, ACROSS_X, h)
        pass_on(1, ACROSS_Y, 1, h)

    def forward_second(h):
        arrived(1, ACROSS_X, h)
        pass_on(1, ACROSS_X, 1, h)
        arrived(0, ACROSS_Y, h)
        pass_on(0, ACROSS_Y, 1, h)

    def forward_last(h):
        arrived(1, DIAG, h)
        pass_on(1, DIAG, 1, h)
        arrived(0, DIAG, h)
        pass_on(0, DIAG, 1, h)

    def other_core(mask, h):
        arrived(0, mask + 1, h)
        arrived(1, mask + 1, h)

    x_arrived(DIAG)
    forward(DIAG, 0, 0)
    forward(DIAG, 1, 0)
    x_arrived(ACROSS_X)
    forward(ACROSS_X, 0, 0)
    send_sum(DIAG, 0, 0, ACROSS_X, 0)
    send_sum(DIAG, 1, 0, ACROSS_Y, 0)
    x_arrived(ACROSS_Y)
    forward(ACROSS_Y, 1, 0)
    send_sum(ACROSS_X, 0, 1, ACROSS_X, 0)
    send_sum(ACROSS_Y, 1, 1, ACROSS_Y, 0)
    forward(ACROSS_Y, 0, 0)
    forward(ACROSS_X, 1, 0)
    x_arrived(OWN)
    forward(OWN, 0, 0)
    forward(OWN, 1, 0)
    forward(DIAG, 0, 1)
    forward(DIAG, 1, 1)
    for h, (base, width) in enumerate(chunks):
        ups[h][...] = up_ref[base : base + width, :].T
    send_sum(ACROSS_Y, 0, 2, ACROSS_Y, 0, extra=0)
    send_sum(ACROSS_X, 1, 2, ACROSS_X, 0, extra=0)
    send_sum(DIAG, 0, 0, ACROSS_X, 1)
    send_sum(DIAG, 1, 0, ACROSS_Y, 1)
    forward(ACROSS_X, 0, 1)
    forward(ACROSS_Y, 1, 1)
    forward(ACROSS_Y, 0, 1)
    forward(ACROSS_X, 1, 1)
    send_sum(ACROSS_X, 0, 1, ACROSS_X, 1)
    send_sum(ACROSS_Y, 1, 1, ACROSS_Y, 1)
    forward(OWN, 0, 1)
    forward(OWN, 1, 1)
    for mask in (OWN, ACROSS_X, ACROSS_Y, DIAG):
        xt[SLOT[mask]] = columns(mask).T
    activate(0)
    send_sum(ACROSS_Y, 0, 2, ACROSS_Y, 1, extra=0)
    send_sum(ACROSS_X, 1, 2, ACROSS_X, 1, extra=0)
    hid[0 : chunks[0][1], :] = hs[0][...].T
    forward_first(0)
    activate(1)
    other_core(OWN, 0)
    back_inputs(OWN, 0)
    back_weights(OWN, 0)
    forward_second(0)
    other_core(ACROSS_X, 0)
    back_inputs(ACROSS_X, 0)
    other_core(ACROSS_Y, 0)
    back_inputs(ACROSS_Y, 0)
    forward_last(0)
    hid[chunks[1][0] : hidden, :] = hs[1][...].T
    stores = [pltpu.make_async_copy(hid, hid_ref, l_s.at[3])]
    stores[0].start()
    back_weights(ACROSS_X, 0)
    forward_first(1)
    back_weights(ACROSS_Y, 0)
    other_core(DIAG, 0)
    back_inputs(DIAG, 0)
    other_core(OWN, 1)
    back_inputs(OWN, 1)
    forward_second(1)
    back_weights(DIAG, 0)

    dot = [jnp.zeros((tokens, 1), jnp.float32)]

    def collect(mask):
        for m in (mask, mask + 1):
            if m:
                remote(ps.at[b], pr.at[at(m)], p_s.at[m], p_r.at[m], m).wait_recv()
        first = chip_start(mask)
        to = first // per

        @pl.when(to != z)
        def _():
            r = (to - z + dp) % dp
            over_dp(pr.at[pl.ds(first, per)], zr.at[z], z_s.at[r], z_r.at[r], to).start()

        for c in range(2):
            j = first + c
            scaled = pr[j].astype(jnp.float32) * un[j]
            dot[0] = dot[0] + jnp.sum(scaled * gs[j], axis=1, keepdims=True)
            gsend[j] = jnp.sum(scaled, axis=0, keepdims=True)

    other_core(ACROSS_X, 1)
    back_inputs(ACROSS_X, 1)
    other_core(ACROSS_Y, 1)
    back_inputs(ACROSS_Y, 1)
    back_weights(OWN, 1)
    collect(OWN)
    forward_last(1)
    back_weights(ACROSS_X, 1)
    other_core(DIAG, 1)
    back_inputs(DIAG, 1)
    collect(ACROSS_X)
    collect(ACROSS_Y)
    back_weights(ACROSS_Y, 1)
    collect(DIAG)
    for m in range(1, 8):
        start(remote(gsend, gsum.at[b], e_s.at[m], e_r.at[m], m))
    dots[...] = jnp.broadcast_to(dot[0], (tokens, tokens)).T[0:8, :]
    for r in range(1, dp):
        start(over_dp(dots, dotr.at[z], d_s.at[r], d_r.at[r], (z + r) % dp))
    back_weights(DIAG, 1)
    for i, (held, out_ref) in enumerate(((ggs, gg_ref), (gus, gu_ref))):
        copy = pltpu.make_async_copy(held, out_ref, l_s.at[4 + i])
        copy.start()
        stores.append(copy)
    total_gain = gsend[...]
    for m in range(1, 8):
        remote(gsend, gsum.at[at(m)], e_s.at[m], e_r.at[m], m).wait_recv()
        total_gain = total_gain + gsum[at(m)]
    gtot[...] = total_gain
    for r in range(1, dp):
        to = (z + r) % dp
        start(over_dp(gtot.at[pl.ds(to * per, per)], gz.at[z], f_s.at[r], f_r.at[r], to))

    for r in range(1, dp):
        source = (z + dp - r) % dp
        over_dp(
            pr.at[pl.ds(0, per)], zr.at[source], z_s.at[r], z_r.at[r], source
        ).wait_recv()
    sums = []
    for jj in range(per):
        j = z * per + jj
        total = pr[j].astype(jnp.float32)
        for r in range(1, dp):
            total = total + zr[(z + r) % dp, jj].astype(jnp.float32)
        sums.append(total)
    total_dot = dots[...]
    for r in range(1, dp):
        source = (z + dp - r) % dp
        over_dp(dots, dotr.at[source], d_s.at[r], d_r.at[r], source).wait_recv()
        total_dot = total_dot + dotr[source]
    means = jnp.broadcast_to(total_dot[0:1, :] / model, (tokens, tokens)).T[:, 0:1]
    root = rm[:, 0:1]
    for jj in range(per):
        j = z * per + jj
        value = (sums[jj] * gs[j] - un[j] * means) / root
        gi_ref[:, jj * block : (jj + 1) * block] = value.astype(jnp.bfloat16)
    total_gain = gtot[pl.ds(z * per, per)]
    for r in range(1, dp):
        source = (z + dp - r) % dp
        over_dp(
            gtot.at[pl.ds(0, per)], gz.at[source], f_s.at[r], f_r.at[r], source
        ).wait_recv()
        total_gain = total_gain + gz[source]
    for jj in range(per):
        ggain_ref[:, jj * block : (jj + 1) * block] = total_gain[jj]

    for copy in sends:
        copy.wait_send()
    for r in range(1, dp):
        over_dp(pr.at[pl.ds(0, per)], zr.at[z], z_s.at[r], z_r.at[r], (z + r) % dp).wait_send()
    for copy in stores:
        copy.wait()


PIECES = 4


def copy_kernel(hid, gg, gu, gi, ggain, hid_ref, gg_ref, gu_ref, gi_ref, ggain_ref, sem):
    rows = gg.shape[0] // PIECES
    copies = []
    for src, dst in ((gg, gg_ref), (gu, gu_ref)):
        for i in range(PIECES):
            part = pl.ds(i * rows, rows)
            copies.append((src.at[part], dst.at[part]))
    copies += [(hid, hid_ref), (gi, gi_ref), (ggain.at[0], ggain_ref)]
    started = []
    for i, (src, dst) in enumerate(copies):
        copy = pltpu.make_async_copy(src, dst, sem.at[i])
        copy.start()
        started.append(copy)
    for copy in started:
        copy.wait()


def by_kernel(dp, inputs, gain, w_gate, w_up, upstream):
    tokens, model = inputs.shape
    block, hidden = w_gate.shape
    per = 8 // dp
    bf16, f32 = jnp.bfloat16, jnp.float32
    vmem = pl.BlockSpec(memory_space=pltpu.VMEM)
    hbm = pl.BlockSpec(memory_space=pl.ANY)

    def dma(*shape):
        return pltpu.SemaphoreType.DMA(shape)

    by_chunk = []
    for _, width in chunks_of(hidden):
        by_chunk += [
            pltpu.VMEM((tokens, width), bf16),
            pltpu.VMEM((tokens, width), bf16),
            pltpu.VMEM((4, 2, 2, tokens, width), bf16),
            pltpu.VMEM((4, 2, tokens, width), bf16),
            pltpu.VMEM((2, 3, tokens, width), bf16),
            pltpu.VMEM((2, 3, tokens, width), bf16),
            pltpu.VMEM((2, 8, tokens, width), bf16),
        ]
    results = pl.pallas_call(
        functools.partial(plane_kernel, dp),
        out_shape=(
            jax.ShapeDtypeStruct((hidden, tokens), bf16),
            jax.ShapeDtypeStruct((block, hidden), f32),
            jax.ShapeDtypeStruct((block, hidden), f32),
            jax.ShapeDtypeStruct((tokens, per * block), bf16),
            jax.ShapeDtypeStruct((1, per * block), f32),
        ),
        in_specs=[vmem, hbm, hbm, hbm, vmem],
        out_specs=(hbm, hbm, hbm, vmem, vmem),
        scratch_shapes=[
            pltpu.VMEM((1, model), f32),
            pltpu.VMEM((8, tokens, block), bf16),
            pltpu.VMEM((8, tokens, block), f32),
            pltpu.VMEM((8, 1, block), f32),
            pltpu.VMEM((tokens, 128), f32),
            pltpu.VMEM((8, tokens, block), bf16),
            pltpu.VMEM((4, block, 2 * tokens), bf16),
            pltpu.VMEM((block, hidden), bf16),
            pltpu.VMEM((block, hidden), bf16),
            pltpu.VMEM((block, hidden), f32),
            pltpu.VMEM((block, hidden), f32),
            pltpu.VMEM((hidden, tokens), bf16),
            pltpu.VMEM((4, 2 * tokens, block), f32),
            pltpu.VMEM((8, tokens, block), bf16),
            pltpu.VMEM((8, tokens, block), bf16),
            pltpu.VMEM((dp, per, tokens, block), bf16),
            pltpu.VMEM((8, tokens), f32),
            pltpu.VMEM((dp, 8, tokens), f32),
            pltpu.VMEM((8, 8, 1, block), f32),
            pltpu.VMEM((8, 1, block), f32),
            pltpu.VMEM((8, 1, block), f32),
            pltpu.VMEM((dp, per, 1, block), f32),
            *by_chunk,
            dma(8), dma(8), dma(2, 4, 2), dma(2, 4, 2), dma(2, 2, 3), dma(2, 2, 3),
            dma(2, 2, 8), dma(2, 2, 8), dma(8), dma(8), dma(dp), dma(dp), dma(dp), dma(dp),
            dma(8), dma(8), dma(dp), dma(dp), dma(6),
        ],
        compiler_params=pltpu.CompilerParams(
            collective_id=0, has_side_effects=True, vmem_limit_bytes=60 * 2**20
        ),
        cost_estimate=pl.CostEstimate(
            flops=48 * tokens * block * hidden * 2,
            bytes_accessed=16 * block * hidden,
            transcendentals=tokens * hidden,
        ),
    )(inputs, gain, w_gate, w_up, upstream.T)
    shapes = [jax.ShapeDtypeStruct(a.shape, a.dtype) for a in results]
    shapes[-1] = jax.ShapeDtypeStruct((per * block,), f32)
    hid, grad_gate, grad_up, grad_input, grad_gain = pl.pallas_call(
        copy_kernel,
        out_shape=shapes,
        in_specs=[hbm] * 5,
        out_specs=[hbm] * 5,
        scratch_shapes=[dma(2 * PIECES + 3)],
        compiler_params=pltpu.CompilerParams(vmem_limit_bytes=60 * 2**20),
    )(*results)
    return hid.T, grad_gate, grad_up, grad_input, grad_gain


def by_collectives(inputs, gain, w_gate, w_up, upstream):
    wide_input = inputs.astype(jnp.float32)
    root_mean = jnp.sqrt(jnp.mean(wide_input * wide_input, axis=1, keepdims=True) + 1e-05)
    unit_input = wide_input / root_mean
    normed = (unit_input * gain).astype(jnp.bfloat16)
    columns = lax.all_to_all(normed, "blk", split_axis=1, concat_axis=0, tiled=True)
    gate_part = jnp.dot(columns, w_gate, preferred_element_type=jnp.float32).astype(jnp.bfloat16)
    up_part = jnp.dot(columns, w_up, preferred_element_type=jnp.float32).astype(jnp.bfloat16)
    gate_pre = lax.psum_scatter(gate_part, "blk", scatter_dimension=0, tiled=True).astype(jnp.float32)
    up_pre = lax.psum_scatter(up_part, "blk", scatter_dimension=0, tiled=True).astype(jnp.float32)
    sigmoid_gate = jax.nn.sigmoid(gate_pre)
    activated = gate_pre * sigmoid_gate
    hidden = (activated * up_pre).astype(jnp.bfloat16)
    upstream_wide = upstream.astype(jnp.float32)
    back_up = (upstream_wide * activated).astype(jnp.bfloat16)
    back_gate = (
        upstream_wide * up_pre * sigmoid_gate * (1.0 + gate_pre * (1.0 - sigmoid_gate))
    ).astype(jnp.bfloat16)
    all_up = lax.all_gather(back_up, "blk", axis=0, tiled=True)
    all_gate = lax.all_gather(back_gate, "blk", axis=0, tiled=True)
    over_tokens = (((0,), (0,)), ((), ()))
    over_hidden = (((1,), (1,)), ((), ()))
    grad_up = lax.dot_general(columns, all_up, over_tokens, preferred_element_type=jnp.float32)
    grad_gate = lax.dot_general(columns, all_gate, over_tokens, preferred_element_type=jnp.float32)
    part = lax.dot_general(
        all_gate, w_gate, over_hidden, preferred_element_type=jnp.float32
    ) + lax.dot_general(all_up, w_up, over_hidden, preferred_element_type=jnp.float32)
    part = lax.all_to_all(
        part.astype(jnp.bfloat16), "blk", split_axis=0, concat_axis=1, tiled=True
    )
    feature_count = inputs.shape[1] // lax.axis_size("dp")
    feature_start = lax.axis_index("dp") * feature_count
    gain_slice = lax.dynamic_slice_in_dim(gain, feature_start, feature_count, 0)
    unit_slice = lax.dynamic_slice_in_dim(unit_input, feature_start, feature_count, 1)
    own_sums = lax.psum_scatter(part, "dp", scatter_dimension=1, tiled=True).astype(jnp.float32)
    token_totals = lax.psum(jnp.sum(own_sums * gain_slice * unit_slice, axis=1), "dp")
    token_means = token_totals[:, None] / inputs.shape[1]
    grad_input = ((own_sums * gain_slice - unit_slice * token_means) / root_mean).astype(
        jnp.bfloat16
    )
    grad_gain = lax.psum(jnp.sum(own_sums * unit_slice, axis=0), "blk")
    return (hidden, grad_gate, grad_up, grad_input, grad_gain)


def solution(mesh):
    dp = mesh.shape["dp"]
    by_chip = mesh.shape["blk"] == 8 and dp == 4
    return jax.shard_map(
        functools.partial(by_kernel, dp) if by_chip else by_collectives,
        mesh=mesh,
        in_specs=(P("blk", None), P(), P("blk", "dp"), P("blk", "dp"), P("blk", "dp")),
        out_specs=(P("blk", "dp"), P("blk", "dp"), P("blk", "dp"), P("blk", "dp"), P("dp")),
        check_vma=False,
    )
```

```python
import functools

import jax
import jax.numpy as jnp
from jax import lax
from jax.experimental import pallas as pl
from jax.experimental.pallas import tpu as pltpu
from jax.sharding import PartitionSpec as P

MESH = pl.DeviceIdType.MESH
ROWS = 16
TILE = 256
DIAG, ACROSS_X, ACROSS_Y, OWN = 6, 2, 4, 0
SLOT = {DIAG: 0, ACROSS_X: 1, ACROSS_Y: 2, OWN: 3}


def chunks_of(hidden):
    first = (hidden // TILE + 2) // 2 * TILE
    return ((0, first), (first, hidden - first))


def plane_kernel(
    dp, x_ref, gain_ref, wg_ref, wu_ref, up_ref,
    hid_ref, gg_ref, gu_ref, gi_ref, ggain_ref,
    gain_row, nb, un, gs, rm, xs, xt, wgs, wus, ggs, gus, hid, pacc, ps, pr, zr, dots, dotr, gsum, gsend, gtot, gz,
    ups0, hs0, pb0, rc0, sbuf0, rbuf0, full0,
    ups1, hs1, pb1, rc1, sbuf1, rbuf1, full1,
    x_s, x_r, c_s, c_r, r_s, r_r, g_s, g_r, p_s, p_r, z_s, z_r, d_s, d_r, e_s, e_r, f_s, f_r, l_s,
):
    b, z = lax.axis_index("blk"), lax.axis_index("dp")
    core, px, py = b % 2, (b // 2) % 2, b // 4
    tokens, model = x_ref.shape
    block, hidden = wgs.shape
    per = 8 // dp
    weights = (wgs, wus)
    chunks = chunks_of(hidden)
    ups, hs, pb, rc = (ups0, ups1), (hs0, hs1), (pb0, pb1), (rc0, rc1)
    sbuf, rbuf, full = (sbuf0, sbuf1), (rbuf0, rbuf1), (full0, full1)

    def tiles(h):
        width = chunks[h][1]
        return [(lo, min(TILE, width - lo)) for lo in range(0, width, TILE)]

    def at(mask):
        return (
            b
            + (1 - 2 * core) * (mask % 2)
            + (2 - 4 * px) * ((mask // 2) % 2)
            + (4 - 8 * py) * (mask // 4)
        )

    def chip_start(mask):
        return at(mask) - core

    def remote(src, dst, send, recv, mask):
        return pltpu.make_async_remote_copy(
            src_ref=src, dst_ref=dst, send_sem=send, recv_sem=recv,
            device_id={"blk": at(mask)}, device_id_type=MESH,
        )

    def over_dp(src, dst, send, recv, to):
        return pltpu.make_async_remote_copy(
            src_ref=src, dst_ref=dst, send_sem=send, recv_sem=recv,
            device_id={"dp": to}, device_id_type=MESH,
        )

    def row_loop(body):
        def step(i, carry):
            body(pl.ds(pl.multiple_of(i * ROWS, ROWS), ROWS))
            return carry

        lax.fori_loop(0, tokens // ROWS, step, 0)

    barrier = pltpu.get_barrier_semaphore()
    for mask in range(1, 8):
        pl.semaphore_signal(barrier, inc=1, device_id={"blk": at(mask)}, device_id_type=MESH)
    for r in range(1, dp):
        pl.semaphore_signal(
            barrier, inc=1, device_id={"dp": (z + r) % dp}, device_id_type=MESH
        )
    loads = [
        pltpu.make_async_copy(wg_ref, wgs, l_s.at[0]),
        pltpu.make_async_copy(wu_ref, wus, l_s.at[1]),
    ]
    for copy in loads:
        copy.start()
    gain_load = pltpu.make_async_copy(gain_ref, gain_row.at[0], l_s.at[2])
    gain_load.start()
    gain_load.wait()
    for j in range(8):
        gs[j] = gain_row[:, j * block : (j + 1) * block]

    def norm_rows(rows):
        wide = x_ref[rows, :].astype(jnp.float32)
        root = jnp.sqrt(jnp.mean(wide * wide, axis=1, keepdims=True) + 1e-05)
        rm[rows, :] = jnp.broadcast_to(root, (ROWS, 128))
        unit = wide / root
        for j in range(8):
            piece = unit[:, j * block : (j + 1) * block]
            un[j, rows, :] = piece
            nb[j, rows, :] = (piece * gs[j]).astype(jnp.bfloat16)

    row_loop(norm_rows)
    pl.semaphore_wait(barrier, 7 + dp - 1)

    sends = []

    def start(copy):
        copy.start()
        sends.append(copy)
        return copy

    def send_normed(mask):
        copy = remote(nb.at[at(mask)], xs.at[b], x_s.at[mask], x_r.at[mask], mask)
        copy.start()
        return copy

    far = [send_normed(mask) for mask in (6, 7)]
    sends.append(send_normed(1))
    xs[b] = nb[b]
    for copy in far:
        copy.wait_send()
    sends.extend(send_normed(mask) for mask in (2, 4, 3, 5))
    for copy in loads:
        copy.wait()

    def columns(mask):
        return xs[pl.ds(chip_start(mask), 2)].reshape(2 * tokens, block)

    def x_arrived(mask):
        for m in (mask, mask + 1):
            if m:
                remote(nb.at[b], xs.at[at(m)], x_s.at[m], x_r.at[m], m).wait_recv()

    c_copies, r_copies = {}, {}

    def forward(mask, mat, h):
        k = SLOT[mask]
        lhs = columns(mask)
        base = chunks[h][0]
        for lo, width in tiles(h):
            out = jnp.dot(
                lhs,
                weights[mat][:, base + lo : base + lo + width],
                preferred_element_type=jnp.float32,
            )
            pb[h][k, mat, :, :, lo : lo + width] = out.astype(jnp.bfloat16).reshape(
                2, tokens, width
            )
        c_copies[k, mat, h] = start(
            remote(
                pb[h].at[k, mat, 1 - core], rc[h].at[k, mat],
                c_s.at[h, k, mat], c_r.at[h, k, mat], 1,
            )
        )

    def send_sum(mask, mat, e, to, h, extra=None):
        k = SLOT[mask]
        c_copies[k, mat, h].wait_recv()
        if extra is not None:
            r_copies[mat, extra, h].wait_recv()

        def rows_sum(rows):
            total = pb[h][k, mat, core, rows, :].astype(jnp.float32)
            total = total + rc[h][k, mat, rows, :].astype(jnp.float32)
            if extra is not None:
                total = total + rbuf[h][mat, extra, rows, :].astype(jnp.float32)
            sbuf[h][mat, e, rows, :] = total.astype(jnp.bfloat16)

        row_loop(rows_sum)
        r_copies[mat, e, h] = start(
            remote(
                sbuf[h].at[mat, e], rbuf[h].at[mat, e],
                r_s.at[h, mat, e], r_r.at[h, mat, e], to,
            )
        )

    def activate(h):
        for mat in (0, 1):
            c_copies[3, mat, h].wait_recv()
            r_copies[mat, 1, h].wait_recv()
            r_copies[mat, 2, h].wait_recv()

        def act_rows(rows):
            pre = []
            for mat in (0, 1):
                total = pb[h][3, mat, core, rows, :].astype(jnp.float32)
                total = total + rc[h][3, mat, rows, :].astype(jnp.float32)
                total = total + rbuf[h][mat, 1, rows, :].astype(jnp.float32)
                pre.append(total + rbuf[h][mat, 2, rows, :].astype(jnp.float32))
            gate_pre, up_pre = pre
            sig = jax.nn.sigmoid(gate_pre)
            activated = gate_pre * sig
            hs[h][rows, :] = (activated * up_pre).astype(jnp.bfloat16)
            wide = ups[h][rows, :].astype(jnp.float32)
            full[h][1, b, rows, :] = (wide * activated).astype(jnp.bfloat16)
            full[h][0, b, rows, :] = (
                wide * up_pre * sig * (1.0 + gate_pre * (1.0 - sig))
            ).astype(jnp.bfloat16)

        row_loop(act_rows)
        pass_on(0, OWN, ACROSS_X, h)
        pass_on(1, OWN, ACROSS_Y, h)
        pass_on(0, OWN, 1, h)
        pass_on(1, OWN, 1, h)

    def second_sends(h):
        pass_on(1, OWN, ACROSS_X, h)
        pass_on(0, OWN, ACROSS_Y, h)

    def pass_on(mat, origin, to, h):
        there = origin ^ to
        t = at(origin)
        start(
            remote(
                full[h].at[mat, t], full[h].at[mat, t],
                g_s.at[h, mat, there], g_r.at[h, mat, there], to,
            )
        )

    def arrived(mat, origin, h):
        t = at(origin)
        remote(
            full[h].at[mat, t], full[h].at[mat, t],
            g_s.at[h, mat, origin], g_r.at[h, mat, origin], 1,
        ).wait_recv()

    def back_inputs(mask, h):
        base, width = chunks[h]
        first = chip_start(mask)
        part = pacc[SLOT[mask]] if h else None
        for mat in (0, 1):
            term = lax.dot_general(
                full[h][mat, pl.ds(first, 2)].reshape(2 * tokens, width),
                weights[mat][:, base : base + width],
                (((1,), (1,)), ((), ())),
                preferred_element_type=jnp.float32,
            )
            part = term if part is None else part + term
        if h == 0:
            pacc[SLOT[mask]] = part
            return
        ps[pl.ds(first, 2)] = part.astype(jnp.bfloat16).reshape(2, tokens, block)
        for m in (mask, mask + 1):
            if m:
                start(remote(ps.at[at(m)], pr.at[b], p_s.at[m], p_r.at[m], m))
            else:
                pr[b] = ps[b]

    def back_weights(mask, h):
        base = chunks[h][0]
        for mat, out_ref in ((0, ggs), (1, gus)):
            for lo, width in tiles(h):
                piece = full[h][mat, pl.ds(chip_start(mask), 2), :, lo : lo + width]
                term = jnp.dot(
                    xt[SLOT[mask]],
                    piece.reshape(2 * tokens, width),
                    preferred_element_type=jnp.float32,
                )
                if mask == OWN:
                    out_ref[:, base + lo : base + lo + width] = term
                else:
                    out_ref[:, base + lo : base + lo + width] += term

    def forward_first(h):
        arrived(0, ACROSS_X, h)
        pass_on(0, ACROSS_X, ACROSS_Y, h)
        pass_on(0, ACROSS_X, 1, h)
        arrived(1, ACROSS_Y, h)
        pass_on(1, ACROSS_Y, ACROSS_X, h)
        pass_on(1, ACROSS_Y, 1, h)

    def forward_second(h):
        arrived(1, ACROSS_X, h)
        pass_on(1, ACROSS_X, 1, h)
        arrived(0, ACROSS_Y, h)
        pass_on(0, ACROSS_Y, 1, h)

    def forward_last(h):
        arrived(1, DIAG, h)
        pass_on(1, DIAG, 1, h)
        arrived(0, DIAG, h)
        pass_on(0, DIAG, 1, h)

    def other_core(mask, h):
        arrived(0, mask + 1, h)
        arrived(1, mask + 1, h)

    x_arrived(DIAG)
    forward(DIAG, 0, 0)
    forward(DIAG, 1, 0)
    x_arrived(ACROSS_X)
    forward(ACROSS_X, 0, 0)
    send_sum(DIAG, 0, 0, ACROSS_X, 0)
    send_sum(DIAG, 1, 0, ACROSS_Y, 0)
    x_arrived(ACROSS_Y)
    forward(ACROSS_Y, 1, 0)
    send_sum(ACROSS_X, 0, 1, ACROSS_X, 0)
    send_sum(ACROSS_Y, 1, 1, ACROSS_Y, 0)
    forward(ACROSS_Y, 0, 0)
    forward(ACROSS_X, 1, 0)
    x_arrived(OWN)
    forward(OWN, 0, 0)
    forward(OWN, 1, 0)
    forward(DIAG, 0, 1)
    forward(DIAG, 1, 1)
    for h, (base, width) in enumerate(chunks):
        ups[h][...] = up_ref[base : base + width, :].T
    send_sum(ACROSS_Y, 0, 2, ACROSS_Y, 0, extra=0)
    send_sum(ACROSS_X, 1, 2, ACROSS_X, 0, extra=0)
    send_sum(DIAG, 0, 0, ACROSS_X, 1)
    send_sum(DIAG, 1, 0, ACROSS_Y, 1)
    forward(ACROSS_X, 0, 1)
    forward(ACROSS_Y, 1, 1)
    forward(ACROSS_Y, 0, 1)
    forward(ACROSS_X, 1, 1)
    send_sum(ACROSS_X, 0, 1, ACROSS_X, 1)
    send_sum(ACROSS_Y, 1, 1, ACROSS_Y, 1)
    forward(OWN, 0, 1)
    forward(OWN, 1, 1)
    for mask in (OWN, ACROSS_X, ACROSS_Y, DIAG):
        xt[SLOT[mask]] = columns(mask).T
    activate(0)
    second_sends(0)
    send_sum(ACROSS_Y, 0, 2, ACROSS_Y, 1, extra=0)
    send_sum(ACROSS_X, 1, 2, ACROSS_X, 1, extra=0)
    hid[0 : chunks[0][1], :] = hs[0][...].T
    forward_first(0)
    activate(1)
    other_core(OWN, 0)
    back_inputs(OWN, 0)
    second_sends(1)
    back_weights(OWN, 0)
    forward_second(0)
    other_core(ACROSS_X, 0)
    back_inputs(ACROSS_X, 0)
    other_core(ACROSS_Y, 0)
    back_inputs(ACROSS_Y, 0)
    forward_last(0)
    hid[chunks[1][0] : hidden, :] = hs[1][...].T
    stores = [pltpu.make_async_copy(hid, hid_ref, l_s.at[3])]
    stores[0].start()
    back_weights(ACROSS_X, 0)
    forward_first(1)
    back_weights(ACROSS_Y, 0)
    other_core(DIAG, 0)
    back_inputs(DIAG, 0)
    other_core(OWN, 1)
    back_inputs(OWN, 1)
    forward_second(1)
    back_weights(DIAG, 0)

    dot = [jnp.zeros((tokens, 1), jnp.float32)]

    def collect(mask):
        for m in (mask, mask + 1):
            if m:
                remote(ps.at[b], pr.at[at(m)], p_s.at[m], p_r.at[m], m).wait_recv()
        first = chip_start(mask)
        to = first // per

        @pl.when(to != z)
        def _():
            r = (to - z + dp) % dp
            over_dp(pr.at[pl.ds(first, per)], zr.at[z], z_s.at[r], z_r.at[r], to).start()

        for c in range(2):
            j = first + c
            scaled = pr[j].astype(jnp.float32) * un[j]
            dot[0] = dot[0] + jnp.sum(scaled * gs[j], axis=1, keepdims=True)
            gsend[j] = jnp.sum(scaled, axis=0, keepdims=True)

    other_core(ACROSS_X, 1)
    back_inputs(ACROSS_X, 1)
    other_core(ACROSS_Y, 1)
    back_inputs(ACROSS_Y, 1)
    back_weights(OWN, 1)
    collect(OWN)
    forward_last(1)
    back_weights(ACROSS_X, 1)
    other_core(DIAG, 1)
    back_inputs(DIAG, 1)
    collect(ACROSS_X)
    collect(ACROSS_Y)
    back_weights(ACROSS_Y, 1)
    collect(DIAG)
    for m in range(1, 8):
        start(remote(gsend, gsum.at[b], e_s.at[m], e_r.at[m], m))
    dots[...] = jnp.broadcast_to(dot[0], (tokens, tokens)).T[0:8, :]
    for r in range(1, dp):
        start(over_dp(dots, dotr.at[z], d_s.at[r], d_r.at[r], (z + r) % dp))
    back_weights(DIAG, 1)
    for i, (held, out_ref) in enumerate(((ggs, gg_ref), (gus, gu_ref))):
        copy = pltpu.make_async_copy(held, out_ref, l_s.at[4 + i])
        copy.start()
        stores.append(copy)
    total_gain = gsend[...]
    for m in range(1, 8):
        remote(gsend, gsum.at[at(m)], e_s.at[m], e_r.at[m], m).wait_recv()
        total_gain = total_gain + gsum[at(m)]
    gtot[...] = total_gain
    for r in range(1, dp):
        to = (z + r) % dp
        start(over_dp(gtot.at[pl.ds(to * per, per)], gz.at[z], f_s.at[r], f_r.at[r], to))

    for r in range(1, dp):
        source = (z + dp - r) % dp
        over_dp(
            pr.at[pl.ds(0, per)], zr.at[source], z_s.at[r], z_r.at[r], source
        ).wait_recv()
    sums = []
    for jj in range(per):
        j = z * per + jj
        total = pr[j].astype(jnp.float32)
        for r in range(1, dp):
            total = total + zr[(z + r) % dp, jj].astype(jnp.float32)
        sums.append(total)
    total_dot = dots[...]
    for r in range(1, dp):
        source = (z + dp - r) % dp
        over_dp(dots, dotr.at[source], d_s.at[r], d_r.at[r], source).wait_recv()
        total_dot = total_dot + dotr[source]
    means = jnp.broadcast_to(total_dot[0:1, :] / model, (tokens, tokens)).T[:, 0:1]
    root = rm[:, 0:1]
    for jj in range(per):
        j = z * per + jj
        value = (sums[jj] * gs[j] - un[j] * means) / root
        gi_ref[:, jj * block : (jj + 1) * block] = value.astype(jnp.bfloat16)
    total_gain = gtot[pl.ds(z * per, per)]
    for r in range(1, dp):
        source = (z + dp - r) % dp
        over_dp(
            gtot.at[pl.ds(0, per)], gz.at[source], f_s.at[r], f_r.at[r], source
        ).wait_recv()
        total_gain = total_gain + gz[source]
    for jj in range(per):
        ggain_ref[:, jj * block : (jj + 1) * block] = total_gain[jj]

    for copy in sends:
        copy.wait_send()
    for r in range(1, dp):
        over_dp(pr.at[pl.ds(0, per)], zr.at[z], z_s.at[r], z_r.at[r], (z + r) % dp).wait_send()
    for copy in stores:
        copy.wait()


PIECES = 4


def copy_kernel(
    hid, gg, gu, gi, ggain, hid_ref, gg_ref, gu_ref, gi_ref, ggain_ref,
    hid_v, gg_v, gu_v, gi_v, ggain_v, in_sem, out_sem,
):
    rows = gg.shape[0] // PIECES
    ways = []
    for i in range(PIECES):
        part = pl.ds(i * rows, rows)
        for src, held, dst in ((gg, gg_v, gg_ref), (gu, gu_v, gu_ref)):
            ways.append((src.at[part], held.at[part], held.at[part], dst.at[part]))
    ways += [
        (hid, hid_v, hid_v, hid_ref),
        (gi, gi_v, gi_v, gi_ref),
        (ggain, ggain_v, ggain_v.at[0], ggain_ref),
    ]
    loads = [pltpu.make_async_copy(w[0], w[1], in_sem.at[i]) for i, w in enumerate(ways)]
    stores = [pltpu.make_async_copy(w[2], w[3], out_sem.at[i]) for i, w in enumerate(ways)]
    for load in loads:
        load.start()
    for load, store in zip(loads, stores):
        load.wait()
        store.start()
    for store in stores:
        store.wait()


def by_kernel(dp, inputs, gain, w_gate, w_up, upstream):
    tokens, model = inputs.shape
    block, hidden = w_gate.shape
    per = 8 // dp
    bf16, f32 = jnp.bfloat16, jnp.float32
    vmem = pl.BlockSpec(memory_space=pltpu.VMEM)
    hbm = pl.BlockSpec(memory_space=pl.ANY)

    def dma(*shape):
        return pltpu.SemaphoreType.DMA(shape)

    by_chunk = []
    for _, width in chunks_of(hidden):
        by_chunk += [
            pltpu.VMEM((tokens, width), bf16),
            pltpu.VMEM((tokens, width), bf16),
            pltpu.VMEM((4, 2, 2, tokens, width), bf16),
            pltpu.VMEM((4, 2, tokens, width), bf16),
            pltpu.VMEM((2, 3, tokens, width), bf16),
            pltpu.VMEM((2, 3, tokens, width), bf16),
            pltpu.VMEM((2, 8, tokens, width), bf16),
        ]
    results = pl.pallas_call(
        functools.partial(plane_kernel, dp),
        out_shape=(
            jax.ShapeDtypeStruct((hidden, tokens), bf16),
            jax.ShapeDtypeStruct((block, hidden), f32),
            jax.ShapeDtypeStruct((block, hidden), f32),
            jax.ShapeDtypeStruct((tokens, per * block), bf16),
            jax.ShapeDtypeStruct((1, per * block), f32),
        ),
        in_specs=[vmem, hbm, hbm, hbm, vmem],
        out_specs=(hbm, hbm, hbm, vmem, vmem),
        scratch_shapes=[
            pltpu.VMEM((1, model), f32),
            pltpu.VMEM((8, tokens, block), bf16),
            pltpu.VMEM((8, tokens, block), f32),
            pltpu.VMEM((8, 1, block), f32),
            pltpu.VMEM((tokens, 128), f32),
            pltpu.VMEM((8, tokens, block), bf16),
            pltpu.VMEM((4, block, 2 * tokens), bf16),
            pltpu.VMEM((block, hidden), bf16),
            pltpu.VMEM((block, hidden), bf16),
            pltpu.VMEM((block, hidden), f32),
            pltpu.VMEM((block, hidden), f32),
            pltpu.VMEM((hidden, tokens), bf16),
            pltpu.VMEM((4, 2 * tokens, block), f32),
            pltpu.VMEM((8, tokens, block), bf16),
            pltpu.VMEM((8, tokens, block), bf16),
            pltpu.VMEM((dp, per, tokens, block), bf16),
            pltpu.VMEM((8, tokens), f32),
            pltpu.VMEM((dp, 8, tokens), f32),
            pltpu.VMEM((8, 8, 1, block), f32),
            pltpu.VMEM((8, 1, block), f32),
            pltpu.VMEM((8, 1, block), f32),
            pltpu.VMEM((dp, per, 1, block), f32),
            *by_chunk,
            dma(8), dma(8), dma(2, 4, 2), dma(2, 4, 2), dma(2, 2, 3), dma(2, 2, 3),
            dma(2, 2, 8), dma(2, 2, 8), dma(8), dma(8), dma(dp), dma(dp), dma(dp), dma(dp),
            dma(8), dma(8), dma(dp), dma(dp), dma(6),
        ],
        compiler_params=pltpu.CompilerParams(
            collective_id=0, has_side_effects=True, vmem_limit_bytes=60 * 2**20
        ),
        cost_estimate=pl.CostEstimate(
            flops=48 * tokens * block * hidden * 2,
            bytes_accessed=16 * block * hidden,
            transcendentals=tokens * hidden,
        ),
    )(inputs, gain, w_gate, w_up, upstream.T)
    shapes = [jax.ShapeDtypeStruct(a.shape, a.dtype) for a in results]
    shapes[-1] = jax.ShapeDtypeStruct((per * block,), f32)
    hid, grad_gate, grad_up, grad_input, grad_gain = pl.pallas_call(
        copy_kernel,
        out_shape=shapes,
        in_specs=[hbm] * 5,
        out_specs=[hbm] * 5,
        scratch_shapes=[
            *(pltpu.VMEM(a.shape, a.dtype) for a in results),
            dma(2 * PIECES + 3),
            dma(2 * PIECES + 3),
        ],
        compiler_params=pltpu.CompilerParams(vmem_limit_bytes=60 * 2**20),
    )(*results)
    return hid.T, grad_gate, grad_up, grad_input, grad_gain


def by_collectives(inputs, gain, w_gate, w_up, upstream):
    wide_input = inputs.astype(jnp.float32)
    root_mean = jnp.sqrt(jnp.mean(wide_input * wide_input, axis=1, keepdims=True) + 1e-05)
    unit_input = wide_input / root_mean
    normed = (unit_input * gain).astype(jnp.bfloat16)
    columns = lax.all_to_all(normed, "blk", split_axis=1, concat_axis=0, tiled=True)
    gate_part = jnp.dot(columns, w_gate, preferred_element_type=jnp.float32).astype(jnp.bfloat16)
    up_part = jnp.dot(columns, w_up, preferred_element_type=jnp.float32).astype(jnp.bfloat16)
    gate_pre = lax.psum_scatter(gate_part, "blk", scatter_dimension=0, tiled=True).astype(jnp.float32)
    up_pre = lax.psum_scatter(up_part, "blk", scatter_dimension=0, tiled=True).astype(jnp.float32)
    sigmoid_gate = jax.nn.sigmoid(gate_pre)
    activated = gate_pre * sigmoid_gate
    hidden = (activated * up_pre).astype(jnp.bfloat16)
    upstream_wide = upstream.astype(jnp.float32)
    back_up = (upstream_wide * activated).astype(jnp.bfloat16)
    back_gate = (
        upstream_wide * up_pre * sigmoid_gate * (1.0 + gate_pre * (1.0 - sigmoid_gate))
    ).astype(jnp.bfloat16)
    all_up = lax.all_gather(back_up, "blk", axis=0, tiled=True)
    all_gate = lax.all_gather(back_gate, "blk", axis=0, tiled=True)
    over_tokens = (((0,), (0,)), ((), ()))
    over_hidden = (((1,), (1,)), ((), ()))
    grad_up = lax.dot_general(columns, all_up, over_tokens, preferred_element_type=jnp.float32)
    grad_gate = lax.dot_general(columns, all_gate, over_tokens, preferred_element_type=jnp.float32)
    part = lax.dot_general(
        all_gate, w_gate, over_hidden, preferred_element_type=jnp.float32
    ) + lax.dot_general(all_up, w_up, over_hidden, preferred_element_type=jnp.float32)
    part = lax.all_to_all(
        part.astype(jnp.bfloat16), "blk", split_axis=0, concat_axis=1, tiled=True
    )
    feature_count = inputs.shape[1] // lax.axis_size("dp")
    feature_start = lax.axis_index("dp") * feature_count
    gain_slice = lax.dynamic_slice_in_dim(gain, feature_start, feature_count, 0)
    unit_slice = lax.dynamic_slice_in_dim(unit_input, feature_start, feature_count, 1)
    own_sums = lax.psum_scatter(part, "dp", scatter_dimension=1, tiled=True).astype(jnp.float32)
    token_totals = lax.psum(jnp.sum(own_sums * gain_slice * unit_slice, axis=1), "dp")
    token_means = token_totals[:, None] / inputs.shape[1]
    grad_input = ((own_sums * gain_slice - unit_slice * token_means) / root_mean).astype(
        jnp.bfloat16
    )
    grad_gain = lax.psum(jnp.sum(own_sums * unit_slice, axis=0), "blk")
    return (hidden, grad_gate, grad_up, grad_input, grad_gain)


def solution(mesh):
    dp = mesh.shape["dp"]
    by_chip = mesh.shape["blk"] == 8 and dp == 4
    return jax.shard_map(
        functools.partial(by_kernel, dp) if by_chip else by_collectives,
        mesh=mesh,
        in_specs=(P("blk", None), P(), P("blk", "dp"), P("blk", "dp"), P("blk", "dp")),
        out_specs=(P("blk", "dp"), P("blk", "dp"), P("blk", "dp"), P("blk", "dp"), P("dp")),
        check_vma=False,
    )
```

```python
import functools

import jax
import jax.numpy as jnp
from jax import lax
from jax.experimental import pallas as pl
from jax.experimental.pallas import tpu as pltpu
from jax.sharding import PartitionSpec as P

MESH = pl.DeviceIdType.MESH
ROWS = 16
TILE = 256
DIAG, ACROSS_X, ACROSS_Y, OWN = 6, 2, 4, 0
SLOT = {DIAG: 0, ACROSS_X: 1, ACROSS_Y: 2, OWN: 3}


def chunks_of(hidden):
    first = (hidden // TILE + 2) // 2 * TILE
    return ((0, first), (first, hidden - first))


def plane_kernel(
    dp, x_hbm, gain_ref, wg_ref, wu_ref, up_hbm,
    hid_ref, gg_ref, gu_ref, gi_ref, ggain_ref,
    x_ref, up_ref, gain_row, nb, un, gs, rm, xs, xt, wgs, wus, ggs, gus, hid, pacc, ps, pr, zr, dots, dotr, gsum, gsend, gtot, gz,
    ups0, hs0, pb0, rc0, sbuf0, rbuf0, full0,
    ups1, hs1, pb1, rc1, sbuf1, rbuf1, full1,
    x_s, x_r, c_s, c_r, r_s, r_r, g_s, g_r, p_s, p_r, z_s, z_r, d_s, d_r, e_s, e_r, f_s, f_r, l_s,
):
    b, z = lax.axis_index("blk"), lax.axis_index("dp")
    core, px, py = b % 2, (b // 2) % 2, b // 4
    tokens, model = x_ref.shape
    block, hidden = wgs.shape
    per = 8 // dp
    weights = (wgs, wus)
    chunks = chunks_of(hidden)
    ups, hs, pb, rc = (ups0, ups1), (hs0, hs1), (pb0, pb1), (rc0, rc1)
    sbuf, rbuf, full = (sbuf0, sbuf1), (rbuf0, rbuf1), (full0, full1)

    def tiles(h):
        width = chunks[h][1]
        return [(lo, min(TILE, width - lo)) for lo in range(0, width, TILE)]

    def at(mask):
        return (
            b
            + (1 - 2 * core) * (mask % 2)
            + (2 - 4 * px) * ((mask // 2) % 2)
            + (4 - 8 * py) * (mask // 4)
        )

    def chip_start(mask):
        return at(mask) - core

    def remote(src, dst, send, recv, mask):
        return pltpu.make_async_remote_copy(
            src_ref=src, dst_ref=dst, send_sem=send, recv_sem=recv,
            device_id={"blk": at(mask)}, device_id_type=MESH,
        )

    def over_dp(src, dst, send, recv, to):
        return pltpu.make_async_remote_copy(
            src_ref=src, dst_ref=dst, send_sem=send, recv_sem=recv,
            device_id={"dp": to}, device_id_type=MESH,
        )

    def row_loop(body, rows=ROWS):
        def step(i, carry):
            body(pl.ds(pl.multiple_of(i * rows, rows), rows))
            return carry

        lax.fori_loop(0, tokens // rows, step, 0)

    loads = [
        pltpu.make_async_copy(src, dst, l_s.at[i])
        for i, (src, dst) in enumerate(
            ((x_hbm, x_ref), (gain_ref, gain_row.at[0]), (wg_ref, wgs), (wu_ref, wus), (up_hbm, up_ref))
        )
    ]
    for copy in loads:
        copy.start()
    barrier = pltpu.get_barrier_semaphore()
    for mask in range(1, 8):
        pl.semaphore_signal(barrier, inc=1, device_id={"blk": at(mask)}, device_id_type=MESH)
    for r in range(1, dp):
        pl.semaphore_signal(
            barrier, inc=1, device_id={"dp": (z + r) % dp}, device_id_type=MESH
        )
    for copy in loads[:2]:
        copy.wait()
    for j in range(8):
        gs[j] = gain_row[:, j * block : (j + 1) * block]

    def norm_rows(rows):
        wide = x_ref[rows, :].astype(jnp.float32)
        root = jnp.sqrt(jnp.mean(wide * wide, axis=1, keepdims=True) + 1e-05)
        rm[rows, :] = jnp.broadcast_to(root, (2 * ROWS, 128))
        unit = wide / root
        for j in range(8):
            piece = unit[:, j * block : (j + 1) * block]
            un[j, rows, :] = piece
            nb[j, rows, :] = (piece * gs[j]).astype(jnp.bfloat16)

    row_loop(norm_rows, 2 * ROWS)
    pl.semaphore_wait(barrier, 7 + dp - 1)

    sends = []

    def start(copy):
        copy.start()
        sends.append(copy)
        return copy

    def send_normed(mask):
        copy = remote(nb.at[at(mask)], xs.at[b], x_s.at[mask], x_r.at[mask], mask)
        copy.start()
        return copy

    far = [send_normed(mask) for mask in (6, 7)]
    sends.append(send_normed(1))
    xs[b] = nb[b]
    for copy in far:
        copy.wait_send()
    sends.extend(send_normed(mask) for mask in (2, 4, 3, 5))
    for copy in loads[2:]:
        copy.wait()

    def columns(mask):
        return xs[pl.ds(chip_start(mask), 2)].reshape(2 * tokens, block)

    def x_arrived(mask):
        for m in (mask, mask + 1):
            if m:
                remote(nb.at[b], xs.at[at(m)], x_s.at[m], x_r.at[m], m).wait_recv()

    c_copies, r_copies = {}, {}

    def forward(mask, mat, h):
        k = SLOT[mask]
        lhs = columns(mask)
        base = chunks[h][0]
        for lo, width in tiles(h):
            out = jnp.dot(
                lhs,
                weights[mat][:, base + lo : base + lo + width],
                preferred_element_type=jnp.float32,
            )
            pb[h][k, mat, :, :, lo : lo + width] = out.astype(jnp.bfloat16).reshape(
                2, tokens, width
            )
        c_copies[k, mat, h] = start(
            remote(
                pb[h].at[k, mat, 1 - core], rc[h].at[k, mat],
                c_s.at[h, k, mat], c_r.at[h, k, mat], 1,
            )
        )

    def send_sum(mask, mat, e, to, h, extra=None):
        k = SLOT[mask]
        c_copies[k, mat, h].wait_recv()
        if extra is not None:
            r_copies[mat, extra, h].wait_recv()

        def rows_sum(rows):
            total = pb[h][k, mat, core, rows, :].astype(jnp.float32)
            total = total + rc[h][k, mat, rows, :].astype(jnp.float32)
            if extra is not None:
                total = total + rbuf[h][mat, extra, rows, :].astype(jnp.float32)
            sbuf[h][mat, e, rows, :] = total.astype(jnp.bfloat16)

        row_loop(rows_sum)
        r_copies[mat, e, h] = start(
            remote(
                sbuf[h].at[mat, e], rbuf[h].at[mat, e],
                r_s.at[h, mat, e], r_r.at[h, mat, e], to,
            )
        )

    def activate(h):
        for mat in (0, 1):
            c_copies[3, mat, h].wait_recv()
            r_copies[mat, 1, h].wait_recv()
            r_copies[mat, 2, h].wait_recv()

        def act_rows(rows):
            pre = []
            for mat in (0, 1):
                total = pb[h][3, mat, core, rows, :].astype(jnp.float32)
                total = total + rc[h][3, mat, rows, :].astype(jnp.float32)
                total = total + rbuf[h][mat, 1, rows, :].astype(jnp.float32)
                pre.append(total + rbuf[h][mat, 2, rows, :].astype(jnp.float32))
            gate_pre, up_pre = pre
            sig = jax.nn.sigmoid(gate_pre)
            activated = gate_pre * sig
            hs[h][rows, :] = (activated * up_pre).astype(jnp.bfloat16)
            wide = ups[h][rows, :].astype(jnp.float32)
            full[h][1, b, rows, :] = (wide * activated).astype(jnp.bfloat16)
            full[h][0, b, rows, :] = (
                wide * up_pre * sig * (1.0 + gate_pre * (1.0 - sig))
            ).astype(jnp.bfloat16)

        row_loop(act_rows)
        pass_on(0, OWN, ACROSS_X, h)
        pass_on(1, OWN, ACROSS_Y, h)
        pass_on(0, OWN, 1, h)
        pass_on(1, OWN, 1, h)

    def second_sends(h):
        pass_on(1, OWN, ACROSS_X, h)
        pass_on(0, OWN, ACROSS_Y, h)

    def pass_on(mat, origin, to, h):
        there = origin ^ to
        t = at(origin)
        start(
            remote(
                full[h].at[mat, t], full[h].at[mat, t],
                g_s.at[h, mat, there], g_r.at[h, mat, there], to,
            )
        )

    def arrived(mat, origin, h):
        t = at(origin)
        remote(
            full[h].at[mat, t], full[h].at[mat, t],
            g_s.at[h, mat, origin], g_r.at[h, mat, origin], 1,
        ).wait_recv()

    def back_inputs(mask, h):
        base, width = chunks[h]
        first = chip_start(mask)
        part = pacc[SLOT[mask]] if h else None
        for mat in (0, 1):
            term = lax.dot_general(
                full[h][mat, pl.ds(first, 2)].reshape(2 * tokens, width),
                weights[mat][:, base : base + width],
                (((1,), (1,)), ((), ())),
                preferred_element_type=jnp.float32,
            )
            part = term if part is None else part + term
        if h == 0:
            pacc[SLOT[mask]] = part
            return
        ps[pl.ds(first, 2)] = part.astype(jnp.bfloat16).reshape(2, tokens, block)
        for m in (mask, mask + 1):
            if m:
                start(remote(ps.at[at(m)], pr.at[b], p_s.at[m], p_r.at[m], m))
            else:
                pr[b] = ps[b]

    def back_weights(mask, h):
        base = chunks[h][0]
        for mat, out_ref in ((0, ggs), (1, gus)):
            for lo, width in tiles(h):
                piece = full[h][mat, pl.ds(chip_start(mask), 2), :, lo : lo + width]
                term = jnp.dot(
                    xt[SLOT[mask]],
                    piece.reshape(2 * tokens, width),
                    preferred_element_type=jnp.float32,
                )
                if mask == OWN:
                    out_ref[:, base + lo : base + lo + width] = term
                else:
                    out_ref[:, base + lo : base + lo + width] += term

    def forward_first(h):
        arrived(0, ACROSS_X, h)
        pass_on(0, ACROSS_X, ACROSS_Y, h)
        pass_on(0, ACROSS_X, 1, h)
        arrived(1, ACROSS_Y, h)
        pass_on(1, ACROSS_Y, ACROSS_X, h)
        pass_on(1, ACROSS_Y, 1, h)

    def forward_second(h):
        arrived(1, ACROSS_X, h)
        pass_on(1, ACROSS_X, 1, h)
        arrived(0, ACROSS_Y, h)
        pass_on(0, ACROSS_Y, 1, h)

    def forward_last(h):
        arrived(1, DIAG, h)
        pass_on(1, DIAG, 1, h)
        arrived(0, DIAG, h)
        pass_on(0, DIAG, 1, h)

    def other_core(mask, h):
        arrived(0, mask + 1, h)
        arrived(1, mask + 1, h)

    x_arrived(DIAG)
    forward(DIAG, 0, 0)
    forward(DIAG, 1, 0)
    x_arrived(ACROSS_X)
    forward(ACROSS_X, 0, 0)
    send_sum(DIAG, 0, 0, ACROSS_X, 0)
    send_sum(DIAG, 1, 0, ACROSS_Y, 0)
    x_arrived(ACROSS_Y)
    forward(ACROSS_Y, 1, 0)
    send_sum(ACROSS_X, 0, 1, ACROSS_X, 0)
    send_sum(ACROSS_Y, 1, 1, ACROSS_Y, 0)
    forward(ACROSS_Y, 0, 0)
    forward(ACROSS_X, 1, 0)
    x_arrived(OWN)
    forward(OWN, 0, 0)
    forward(OWN, 1, 0)
    forward(DIAG, 0, 1)
    forward(DIAG, 1, 1)
    for h, (base, width) in enumerate(chunks):
        ups[h][...] = up_ref[base : base + width, :].T
    send_sum(ACROSS_Y, 0, 2, ACROSS_Y, 0, extra=0)
    send_sum(ACROSS_X, 1, 2, ACROSS_X, 0, extra=0)
    send_sum(DIAG, 0, 0, ACROSS_X, 1)
    send_sum(DIAG, 1, 0, ACROSS_Y, 1)
    forward(ACROSS_X, 0, 1)
    forward(ACROSS_Y, 1, 1)
    forward(ACROSS_Y, 0, 1)
    forward(ACROSS_X, 1, 1)
    send_sum(ACROSS_X, 0, 1, ACROSS_X, 1)
    send_sum(ACROSS_Y, 1, 1, ACROSS_Y, 1)
    forward(OWN, 0, 1)
    forward(OWN, 1, 1)
    for mask in (OWN, ACROSS_X, ACROSS_Y, DIAG):
        xt[SLOT[mask]] = columns(mask).T
    activate(0)
    second_sends(0)
    send_sum(ACROSS_Y, 0, 2, ACROSS_Y, 1, extra=0)
    send_sum(ACROSS_X, 1, 2, ACROSS_X, 1, extra=0)
    hid[0 : chunks[0][1], :] = hs[0][...].T
    forward_first(0)
    activate(1)
    other_core(OWN, 0)
    back_inputs(OWN, 0)
    second_sends(1)
    back_weights(OWN, 0)
    forward_second(0)
    other_core(ACROSS_X, 0)
    back_inputs(ACROSS_X, 0)
    other_core(ACROSS_Y, 0)
    back_inputs(ACROSS_Y, 0)
    forward_last(0)
    hid[chunks[1][0] : hidden, :] = hs[1][...].T
    stores = [pltpu.make_async_copy(hid, hid_ref, l_s.at[5])]
    stores[0].start()
    back_weights(ACROSS_X, 0)
    forward_first(1)
    back_weights(ACROSS_Y, 0)
    other_core(DIAG, 0)
    back_inputs(DIAG, 0)
    other_core(OWN, 1)
    back_inputs(OWN, 1)
    forward_second(1)
    back_weights(DIAG, 0)

    dot = [jnp.zeros((tokens, 1), jnp.float32)]

    def collect(mask):
        for m in (mask, mask + 1):
            if m:
                remote(ps.at[b], pr.at[at(m)], p_s.at[m], p_r.at[m], m).wait_recv()
        first = chip_start(mask)
        to = first // per

        @pl.when(to != z)
        def _():
            r = (to - z + dp) % dp
            over_dp(pr.at[pl.ds(first, per)], zr.at[z], z_s.at[r], z_r.at[r], to).start()

        for c in range(2):
            j = first + c
            scaled = pr[j].astype(jnp.float32) * un[j]
            dot[0] = dot[0] + jnp.sum(scaled * gs[j], axis=1, keepdims=True)
            gsend[j] = jnp.sum(scaled, axis=0, keepdims=True)

    other_core(ACROSS_X, 1)
    back_inputs(ACROSS_X, 1)
    other_core(ACROSS_Y, 1)
    back_inputs(ACROSS_Y, 1)
    back_weights(OWN, 1)
    collect(OWN)
    forward_last(1)
    back_weights(ACROSS_X, 1)
    other_core(DIAG, 1)
    back_inputs(DIAG, 1)
    collect(ACROSS_X)
    collect(ACROSS_Y)
    back_weights(ACROSS_Y, 1)
    collect(DIAG)
    for m in range(1, 8):
        start(remote(gsend, gsum.at[b], e_s.at[m], e_r.at[m], m))
    dots[...] = jnp.broadcast_to(dot[0], (tokens, tokens)).T[0:8, :]
    for r in range(1, dp):
        start(over_dp(dots, dotr.at[z], d_s.at[r], d_r.at[r], (z + r) % dp))
    back_weights(DIAG, 1)
    for i, (held, out_ref) in enumerate(((ggs, gg_ref), (gus, gu_ref))):
        copy = pltpu.make_async_copy(held, out_ref, l_s.at[6 + i])
        copy.start()
        stores.append(copy)
    total_gain = gsend[...]
    for m in range(1, 8):
        remote(gsend, gsum.at[at(m)], e_s.at[m], e_r.at[m], m).wait_recv()
        total_gain = total_gain + gsum[at(m)]
    gtot[...] = total_gain
    for r in range(1, dp):
        to = (z + r) % dp
        start(over_dp(gtot.at[pl.ds(to * per, per)], gz.at[z], f_s.at[r], f_r.at[r], to))

    for r in range(1, dp):
        source = (z + dp - r) % dp
        over_dp(
            pr.at[pl.ds(0, per)], zr.at[source], z_s.at[r], z_r.at[r], source
        ).wait_recv()
    sums = []
    for jj in range(per):
        j = z * per + jj
        total = pr[j].astype(jnp.float32)
        for r in range(1, dp):
            total = total + zr[(z + r) % dp, jj].astype(jnp.float32)
        sums.append(total)
    total_dot = dots[...]
    for r in range(1, dp):
        source = (z + dp - r) % dp
        over_dp(dots, dotr.at[source], d_s.at[r], d_r.at[r], source).wait_recv()
        total_dot = total_dot + dotr[source]
    means = jnp.broadcast_to(total_dot[0:1, :] / model, (tokens, tokens)).T[:, 0:1]
    root = rm[:, 0:1]
    for jj in range(per):
        j = z * per + jj
        value = (sums[jj] * gs[j] - un[j] * means) / root
        gi_ref[:, jj * block : (jj + 1) * block] = value.astype(jnp.bfloat16)
    total_gain = gtot[pl.ds(z * per, per)]
    for r in range(1, dp):
        source = (z + dp - r) % dp
        over_dp(
            gtot.at[pl.ds(0, per)], gz.at[source], f_s.at[r], f_r.at[r], source
        ).wait_recv()
        total_gain = total_gain + gz[source]
    for jj in range(per):
        ggain_ref[:, jj * block : (jj + 1) * block] = total_gain[jj]

    for copy in sends:
        copy.wait_send()
    for r in range(1, dp):
        over_dp(pr.at[pl.ds(0, per)], zr.at[z], z_s.at[r], z_r.at[r], (z + r) % dp).wait_send()
    for copy in stores:
        copy.wait()


PIECES = 4


def copy_kernel(
    hid, gg, gu, gi, ggain, hid_ref, gg_ref, gu_ref, gi_ref, ggain_ref,
    hid_v, gg_v, gu_v, gi_v, ggain_v, in_sem, out_sem,
):
    rows = gg.shape[0] // PIECES
    ways = []
    for i in range(PIECES):
        part = pl.ds(i * rows, rows)
        for src, held, dst in ((gg, gg_v, gg_ref), (gu, gu_v, gu_ref)):
            ways.append((src.at[part], held.at[part], held.at[part], dst.at[part]))
    ways += [
        (hid, hid_v, hid_v, hid_ref),
        (gi, gi_v, gi_v, gi_ref),
        (ggain, ggain_v, ggain_v.at[0], ggain_ref),
    ]
    loads = [pltpu.make_async_copy(w[0], w[1], in_sem.at[i]) for i, w in enumerate(ways)]
    stores = [pltpu.make_async_copy(w[2], w[3], out_sem.at[i]) for i, w in enumerate(ways)]
    for load in loads:
        load.start()
    for load, store in zip(loads, stores):
        load.wait()
        store.start()
    for store in stores:
        store.wait()


def by_kernel(dp, inputs, gain, w_gate, w_up, upstream):
    tokens, model = inputs.shape
    block, hidden = w_gate.shape
    per = 8 // dp
    bf16, f32 = jnp.bfloat16, jnp.float32
    vmem = pl.BlockSpec(memory_space=pltpu.VMEM)
    hbm = pl.BlockSpec(memory_space=pl.ANY)

    def dma(*shape):
        return pltpu.SemaphoreType.DMA(shape)

    by_chunk = []
    for _, width in chunks_of(hidden):
        by_chunk += [
            pltpu.VMEM((tokens, width), bf16),
            pltpu.VMEM((tokens, width), bf16),
            pltpu.VMEM((4, 2, 2, tokens, width), bf16),
            pltpu.VMEM((4, 2, tokens, width), bf16),
            pltpu.VMEM((2, 3, tokens, width), bf16),
            pltpu.VMEM((2, 3, tokens, width), bf16),
            pltpu.VMEM((2, 8, tokens, width), bf16),
        ]
    results = pl.pallas_call(
        functools.partial(plane_kernel, dp),
        out_shape=(
            jax.ShapeDtypeStruct((hidden, tokens), bf16),
            jax.ShapeDtypeStruct((block, hidden), f32),
            jax.ShapeDtypeStruct((block, hidden), f32),
            jax.ShapeDtypeStruct((tokens, per * block), bf16),
            jax.ShapeDtypeStruct((1, per * block), f32),
        ),
        in_specs=[hbm] * 5,
        out_specs=(hbm, hbm, hbm, vmem, vmem),
        scratch_shapes=[
            pltpu.VMEM((tokens, model), bf16),
            pltpu.VMEM((hidden, tokens), bf16),
            pltpu.VMEM((1, model), f32),
            pltpu.VMEM((8, tokens, block), bf16),
            pltpu.VMEM((8, tokens, block), f32),
            pltpu.VMEM((8, 1, block), f32),
            pltpu.VMEM((tokens, 128), f32),
            pltpu.VMEM((8, tokens, block), bf16),
            pltpu.VMEM((4, block, 2 * tokens), bf16),
            pltpu.VMEM((block, hidden), bf16),
            pltpu.VMEM((block, hidden), bf16),
            pltpu.VMEM((block, hidden), f32),
            pltpu.VMEM((block, hidden), f32),
            pltpu.VMEM((hidden, tokens), bf16),
            pltpu.VMEM((4, 2 * tokens, block), f32),
            pltpu.VMEM((8, tokens, block), bf16),
            pltpu.VMEM((8, tokens, block), bf16),
            pltpu.VMEM((dp, per, tokens, block), bf16),
            pltpu.VMEM((8, tokens), f32),
            pltpu.VMEM((dp, 8, tokens), f32),
            pltpu.VMEM((8, 8, 1, block), f32),
            pltpu.VMEM((8, 1, block), f32),
            pltpu.VMEM((8, 1, block), f32),
            pltpu.VMEM((dp, per, 1, block), f32),
            *by_chunk,
            dma(8), dma(8), dma(2, 4, 2), dma(2, 4, 2), dma(2, 2, 3), dma(2, 2, 3),
            dma(2, 2, 8), dma(2, 2, 8), dma(8), dma(8), dma(dp), dma(dp), dma(dp), dma(dp),
            dma(8), dma(8), dma(dp), dma(dp), dma(8),
        ],
        compiler_params=pltpu.CompilerParams(
            collective_id=0, has_side_effects=True, vmem_limit_bytes=60 * 2**20
        ),
        cost_estimate=pl.CostEstimate(
            flops=48 * tokens * block * hidden * 2,
            bytes_accessed=16 * block * hidden,
            transcendentals=tokens * hidden,
        ),
    )(inputs, gain, w_gate, w_up, upstream.T)
    shapes = [jax.ShapeDtypeStruct(a.shape, a.dtype) for a in results]
    shapes[-1] = jax.ShapeDtypeStruct((per * block,), f32)
    hid, grad_gate, grad_up, grad_input, grad_gain = pl.pallas_call(
        copy_kernel,
        out_shape=shapes,
        in_specs=[hbm] * 5,
        out_specs=[hbm] * 5,
        scratch_shapes=[
            *(pltpu.VMEM(a.shape, a.dtype) for a in results),
            dma(2 * PIECES + 3),
            dma(2 * PIECES + 3),
        ],
        compiler_params=pltpu.CompilerParams(vmem_limit_bytes=60 * 2**20),
    )(*results)
    return hid.T, grad_gate, grad_up, grad_input, grad_gain


def by_collectives(inputs, gain, w_gate, w_up, upstream):
    wide_input = inputs.astype(jnp.float32)
    root_mean = jnp.sqrt(jnp.mean(wide_input * wide_input, axis=1, keepdims=True) + 1e-05)
    unit_input = wide_input / root_mean
    normed = (unit_input * gain).astype(jnp.bfloat16)
    columns = lax.all_to_all(normed, "blk", split_axis=1, concat_axis=0, tiled=True)
    gate_part = jnp.dot(columns, w_gate, preferred_element_type=jnp.float32).astype(jnp.bfloat16)
    up_part = jnp.dot(columns, w_up, preferred_element_type=jnp.float32).astype(jnp.bfloat16)
    gate_pre = lax.psum_scatter(gate_part, "blk", scatter_dimension=0, tiled=True).astype(jnp.float32)
    up_pre = lax.psum_scatter(up_part, "blk", scatter_dimension=0, tiled=True).astype(jnp.float32)
    sigmoid_gate = jax.nn.sigmoid(gate_pre)
    activated = gate_pre * sigmoid_gate
    hidden = (activated * up_pre).astype(jnp.bfloat16)
    upstream_wide = upstream.astype(jnp.float32)
    back_up = (upstream_wide * activated).astype(jnp.bfloat16)
    back_gate = (
        upstream_wide * up_pre * sigmoid_gate * (1.0 + gate_pre * (1.0 - sigmoid_gate))
    ).astype(jnp.bfloat16)
    all_up = lax.all_gather(back_up, "blk", axis=0, tiled=True)
    all_gate = lax.all_gather(back_gate, "blk", axis=0, tiled=True)
    over_tokens = (((0,), (0,)), ((), ()))
    over_hidden = (((1,), (1,)), ((), ()))
    grad_up = lax.dot_general(columns, all_up, over_tokens, preferred_element_type=jnp.float32)
    grad_gate = lax.dot_general(columns, all_gate, over_tokens, preferred_element_type=jnp.float32)
    part = lax.dot_general(
        all_gate, w_gate, over_hidden, preferred_element_type=jnp.float32
    ) + lax.dot_general(all_up, w_up, over_hidden, preferred_element_type=jnp.float32)
    part = lax.all_to_all(
        part.astype(jnp.bfloat16), "blk", split_axis=0, concat_axis=1, tiled=True
    )
    feature_count = inputs.shape[1] // lax.axis_size("dp")
    feature_start = lax.axis_index("dp") * feature_count
    gain_slice = lax.dynamic_slice_in_dim(gain, feature_start, feature_count, 0)
    unit_slice = lax.dynamic_slice_in_dim(unit_input, feature_start, feature_count, 1)
    own_sums = lax.psum_scatter(part, "dp", scatter_dimension=1, tiled=True).astype(jnp.float32)
    token_totals = lax.psum(jnp.sum(own_sums * gain_slice * unit_slice, axis=1), "dp")
    token_means = token_totals[:, None] / inputs.shape[1]
    grad_input = ((own_sums * gain_slice - unit_slice * token_means) / root_mean).astype(
        jnp.bfloat16
    )
    grad_gain = lax.psum(jnp.sum(own_sums * unit_slice, axis=0), "blk")
    return (hidden, grad_gate, grad_up, grad_input, grad_gain)


def solution(mesh):
    dp = mesh.shape["dp"]
    by_chip = mesh.shape["blk"] == 8 and dp == 4
    return jax.shard_map(
        functools.partial(by_kernel, dp) if by_chip else by_collectives,
        mesh=mesh,
        in_specs=(P("blk", None), P(), P("blk", "dp"), P("blk", "dp"), P("blk", "dp")),
        out_specs=(P("blk", "dp"), P("blk", "dp"), P("blk", "dp"), P("blk", "dp"), P("dp")),
        check_vma=False,
    )
```
